256 devices in a mesh: rep: 16 (over y, x), con: 16 (over z, core).
Axes of the slice: x: 4, y: 4, z: 8, core: 2. Of those that a mesh axis runs over, the one named last changes fastest.
Arguments:
- audio_hidden: bfloat16 [40960, 1280], P(('rep', 'con')), may hold values from -6 to 6
- score_hidden: bfloat16 [40960, 1280], P(('rep', 'con')), may hold values from -6 to 6
- audio_proj: bfloat16 [40960, 1024], P(('rep', 'con')), may hold values from -300 to 300
- score_proj: bfloat16 [40960, 1024], P(('rep', 'con')), may hold values from -300 to 300
- labels: int32 [16, 2560], P('rep', 'con'), may hold values from 0 to 2559, as said below
- q_seed: float32 [1024, 64], replicated, may hold values from -6 to 6
- err_audio: float32 [16, 1280, 1024], P('rep', 'con'), may hold values from -4 to 4
- err_score: float32 [16, 1280, 1024], P('rep', 'con'), may hold values from -4 to 4
Outputs:
- p_audio: float32 [1280, 64], P('con')
- q_audio: float32 [1024, 64], replicated
- new_err_audio: float32 [16, 1280, 1024], P('rep', 'con')
- p_score: float32 [1280, 64], P('con')
- q_score: float32 [1024, 64], replicated
- new_err_score: float32 [16, 1280, 1024], P('rep', 'con')
The draws below stay inside these ranges and needn't reach their ends.
Inputs may be any that keep to these rules, and one draw needn't show every extreme that they name: Each row of labels is a permutation of 0 to 2559: audio row i of replica r pairs with score row labels[r, i] of the same replica.
All inputs are finite; a program needn't handle non-finite values.
Results may differ from the reference program's by a relative error of at most 0.00057.
Values may be sent and summed in bfloat16 or wider, within the bound.
A program may use at most 64 MiB of HBM per device.

```python
import math
import jax
import jax.numpy as jnp
from jax import lax

D = 1280
E = 1024
RANK = 64
GROUP = 2560
TOTAL = 40960
N_REP = 16


def pair_draw(key):
    perm_keys = jax.random.split(jax.random.fold_in(key, 101), N_REP)
    pairs = jax.vmap(lambda k: jax.random.permutation(k, GROUP))(perm_keys).astype(jnp.int32)
    shared = jax.random.normal(jax.random.fold_in(key, 102), (N_REP, GROUP, E), jnp.float32)
    column = jnp.exp(jax.random.uniform(jax.random.fold_in(key, 103), (E,), jnp.float32, 0.0, math.log(10.0)))
    return (pairs, shared, column)


def draw_labels(key, part):
    pairs, shared, column = pair_draw(key)
    return pairs


def draw_audio_proj(key, part):
    pairs, shared, column = pair_draw(key)
    key = jax.random.fold_in(key, 1)
    noise = 1.6 * jax.random.normal(jax.random.fold_in(key, 2), (TOTAL, E), jnp.float32)
    scales = jnp.exp(jax.random.uniform(jax.random.fold_in(key, 3), (TOTAL, 1), jnp.float32, 0.0, math.log(10.0)))
    values = (shared.reshape(TOTAL, E) + noise) * column[None, :] * scales
    return jnp.clip(values, -300.0, 300.0).astype(jnp.bfloat16)


def draw_score_proj(key, part):
    pairs, shared, column = pair_draw(key)
    key = jax.random.fold_in(key, 5)
    placed = jax.vmap(lambda rows, order: jnp.zeros_like(rows).at[order].set(rows))(shared, pairs)
    noise = 1.6 * jax.random.normal(jax.random.fold_in(key, 2), (TOTAL, E), jnp.float32)
    scales = jnp.exp(jax.random.uniform(jax.random.fold_in(key, 3), (TOTAL, 1), jnp.float32, 0.0, math.log(10.0)))
    values = (placed.reshape(TOTAL, E) + noise) * column[None, :] * scales
    return jnp.clip(values, -300.0, 300.0).astype(jnp.bfloat16)


def steps_of(own_key, extent, cuts, low, high):
    def one(dim, parts):
        steps = jax.random.uniform(jax.random.fold_in(jax.random.fold_in(own_key, 6), dim), (parts,), jnp.float32, low / len(cuts), high / len(cuts))
        return jnp.repeat(jnp.exp(steps), extent[dim] // parts).reshape((-1,) + (1,) * (len(extent) - dim - 1))

    factor_of = one(*cuts[0])
    for cut in cuts[1:]:
        factor_of = factor_of * one(*cut)
    return factor_of


def normal_values(own_key, extent, scale, limit, cuts=(), kind=jnp.bfloat16):
    drawn = scale * jax.random.normal(own_key, extent, jnp.float32)
    if cuts:
        drawn = drawn * steps_of(own_key, extent, cuts, -0.22, 0.18)
    return jnp.clip(drawn, -limit, limit).astype(kind)


def setup_inputs(seed: int = 0) -> dict:
    key_of = jax.random.split(jax.random.key(seed), 9)
    return {
        "audio_hidden": normal_values(key_of[0], (TOTAL, D), 1.0, 6.0, ((0, 256),)),
        "score_hidden": normal_values(key_of[1], (TOTAL, D), 1.0, 6.0, ((0, 256),)),
        "audio_proj": draw_audio_proj(jax.random.fold_in(key_of[8], 71), 0),
        "score_proj": draw_score_proj(jax.random.fold_in(key_of[8], 71), 0),
        "labels": draw_labels(jax.random.fold_in(key_of[8], 71), 0),
        "q_seed": normal_values(key_of[5], (E, RANK), 1.0, 6.0, (), jnp.float32),
        "err_audio": normal_values(key_of[6], (N_REP, D, E), 0.5, 4.0, ((0, 16), (1, 16)), jnp.float32),
        "err_score": normal_values(key_of[7], (N_REP, D, E), 0.5, 4.0, ((0, 16), (1, 16)), jnp.float32),
    }


logit_scale = 30.0

def normalize(proj):
    values = proj.astype(jnp.float32)
    norm = jnp.sqrt(lax.optimization_barrier(jnp.sum(values * values, axis=1, keepdims=True)) + 1e-06)
    return (values / norm, norm)

def orthonormal(matrix):
    count = matrix.shape[1]

    def column_step(k, basis):
        column = lax.dynamic_slice_in_dim(matrix, k, 1, 1)
        coeffs = jnp.dot(basis.T, column, precision=lax.Precision.HIGHEST)
        column = column - jnp.dot(basis, coeffs, precision=lax.Precision.HIGHEST)
        column = column / jnp.sqrt(jnp.sum(column * column) + 1e-06)
        return lax.dynamic_update_slice_in_dim(basis, column, k, 1)
    return lax.fori_loop(0, count, column_step, jnp.zeros(matrix.shape, jnp.float32))

def replica_grads(pieces):
    hidden_a, hidden_b, proj_a, proj_b, pairs = pieces
    unit_a, norm_a = normalize(proj_a)
    unit_b, norm_b = normalize(proj_b)
    emb_a = unit_a.astype(jnp.bfloat16)
    emb_b = unit_b.astype(jnp.bfloat16)
    logits = logit_scale * jnp.dot(emb_a, emb_b.T, preferred_element_type=jnp.float32)
    row_lse = jnp.log(lax.optimization_barrier(jnp.sum(jnp.exp(logits), axis=1)))
    col_lse = jnp.log(lax.optimization_barrier(jnp.sum(jnp.exp(logits), axis=0)))
    columns = jnp.arange(logits.shape[1], dtype=jnp.int32)
    onehot = (pairs[:, None] == columns[None, :]).astype(jnp.float32)
    weights = 0.5 * (jnp.exp(logits - row_lse[:, None]) + jnp.exp(logits - col_lse[None, :])) - onehot
    weights = weights.astype(jnp.bfloat16)
    grad_ea = logit_scale * jnp.dot(weights, emb_b, preferred_element_type=jnp.float32)
    grad_eb = logit_scale * jnp.dot(weights.T, emb_a, preferred_element_type=jnp.float32)
    dz_a = ((grad_ea - unit_a * lax.optimization_barrier(jnp.sum(unit_a * grad_ea, axis=1, keepdims=True))) / norm_a).astype(jnp.bfloat16)
    dz_b = ((grad_eb - unit_b * lax.optimization_barrier(jnp.sum(unit_b * grad_eb, axis=1, keepdims=True))) / norm_b).astype(jnp.bfloat16)
    grad_a = jnp.dot(hidden_a.T, dz_a, preferred_element_type=jnp.float32)
    grad_b = jnp.dot(hidden_b.T, dz_b, preferred_element_type=jnp.float32)
    return (grad_a, grad_b)

def compress(memory, q_seed):
    summed = lax.optimization_barrier(jnp.sum(memory, axis=0))
    left = jnp.dot(summed, q_seed, precision=lax.Precision.HIGHEST)
    p_hat = orthonormal(left)
    right = jnp.dot(summed.T, p_hat, precision=lax.Precision.HIGHEST) / N_REP
    update = jnp.dot(p_hat, right.T, precision=lax.Precision.HIGHEST)
    return (p_hat, right, memory - update[None])

def reference(audio_hidden, score_hidden, audio_proj, score_proj, labels, q_seed, err_audio, err_score):
    pieces = (audio_hidden.reshape(N_REP, GROUP, D), score_hidden.reshape(N_REP, GROUP, D), audio_proj.reshape(N_REP, GROUP, E), score_proj.reshape(N_REP, GROUP, E), labels)
    grad_a, grad_b = lax.map(replica_grads, pieces)
    p_audio, q_audio, new_err_audio = compress(grad_a + err_audio, q_seed)
    p_score, q_score, new_err_score = compress(grad_b + err_score, q_seed)
    return (p_audio, q_audio, new_err_audio, p_score, q_score, new_err_score)
```

```python
import functools

import jax
import jax.numpy as jnp
from jax import lax
from jax.experimental import pallas as pl
from jax.experimental.pallas import tpu as pltpu
from jax.sharding import PartitionSpec as P

MESH = pl.DeviceIdType.MESH
logit_scale = 30.0
NORM_EPS = 1e-06
NT = (((1,), (1,)), ((), ()))
TN = (((0,), (0,)), ((), ()))
NN = (((1,), (0,)), ((), ()))
HIGH = lax.Precision.HIGHEST

SLOT_OF = (0, 1, 3, 5, 7, 6, 4, 2)
BEHIND = (0, 1, 7, 2, 6, 3, 5, 4)
RING = (
    ((1, 0), (1, 1), (2, 0), (2, 1), (3, 0), (3, 1), (4, 0)),
    ((1, 1), (1, 0), (2, 1), (2, 0), (3, 1), (3, 0), (4, 1)),
)


def exact(left, right, dims):
    return lax.dot_general(
        left, right, dims, precision=HIGH, preferred_element_type=jnp.float32
    )


def grads_kernel(
    n_z, proj_a, proj_b, labels, hidden_a, hidden_b, err_a, err_b,
    mem_ref,
    raw, emb, logit, weight, grad, row_sum, col_sum, row_info, col_id, lab, stage, hid, err,
    ring_send, ring_recv, sib_send, sib_recv, lab_send, lab_recv, hid_send, hid_recv,
    err_send, err_recv, local_sem,
):
    tok = proj_a.shape[0]
    chip = 2 * tok
    width = proj_a.shape[1]
    group = raw.shape[1]
    feat = hid.shape[1]
    slab = err_a.shape[1]
    rep = lax.axis_index("rep")
    con = lax.axis_index("con")
    z = con // 2
    core = lax.rem(con, 2)
    other = 1 - core

    def device(ahead, cross):
        where = lax.rem(z + ahead, n_z)
        return (rep, where * 2 + (other if cross else core))

    partners = [(o, r) for o in range(n_z) for r in range(2) if (o, r) != (0, 0)]

    projs = (proj_a, proj_b)
    loads = [
        pltpu.make_async_copy(projs[t], raw.at[t, pl.ds(0, tok), :], local_sem.at[t])
        for t in range(2)
    ]
    for load in loads:
        load.start()
    errs = (err_a, err_b)

    barrier = pltpu.get_barrier_semaphore()
    for o, r in partners:
        pl.semaphore_signal(barrier, inc=1, device_id=device(o, r), device_id_type=MESH)
    pl.semaphore_wait(barrier, len(partners))
    for load in loads:
        load.wait()

    def ring(way, n):
        dist, t = RING[way][n]
        source = SLOT_OF[dist - 1] if way == 0 else SLOT_OF[(n_z - dist + 1) % n_z]
        target = SLOT_OF[dist] if way == 0 else SLOT_OF[n_z - dist]
        return pltpu.make_async_remote_copy(
            src_ref=raw.at[t, pl.ds(source * chip, tok), :],
            dst_ref=raw.at[t, pl.ds(target * chip, tok), :],
            send_sem=ring_send.at[way, n],
            recv_sem=ring_recv.at[way, n],
            device_id=device(1 if way == 0 else n_z - 1, 0),
            device_id_type=MESH,
        )

    def sib(way, n):
        if n < 0:
            slot, t, index = 0, way, 7
        else:
            dist, t = RING[way][n]
            slot, index = (SLOT_OF[dist] if way == 0 else SLOT_OF[n_z - dist]), n
        return pltpu.make_async_remote_copy(
            src_ref=raw.at[t, pl.ds(slot * chip, tok), :],
            dst_ref=raw.at[t, pl.ds(slot * chip + tok, tok), :],
            send_sem=sib_send.at[way, index],
            recv_sem=sib_recv.at[way, index],
            device_id=device(0, 1),
            device_id_type=MESH,
        )

    def label_copy(o, r):
        return pltpu.make_async_remote_copy(
            src_ref=labels,
            dst_ref=lab.at[SLOT_OF[o], r],
            send_sem=lab_send.at[o, r],
            recv_sem=lab_recv.at[o, r],
            device_id=device(o, r),
            device_id_type=MESH,
        )

    def hidden_copy(o, r):
        return pltpu.make_async_remote_copy(
            src_ref=stage.at[other if r else core, lax.rem(z + o, n_z)],
            dst_ref=hid.at[pl.ds(SLOT_OF[o] * chip + r * tok, tok), :],
            send_sem=hid_send.at[o, r],
            recv_sem=hid_recv.at[o, r],
            device_id=device(o, r),
            device_id_type=MESH,
        )

    def err_copy(t):
        return pltpu.make_async_remote_copy(
            src_ref=errs[t].at[0],
            dst_ref=err.at[1],
            send_sem=err_send,
            recv_sem=err_recv,
            device_id=device(0, 1),
            device_id_type=MESH,
        )

    def err_local(t):
        return pltpu.make_async_copy(errs[t].at[0], err.at[0], local_sem.at[2])

    def normalize(slot, cross, t):
        rows = pl.ds(slot * chip + cross * tok, tok)
        values = raw[t, rows, :].astype(jnp.float32)
        inverse = lax.rsqrt(jnp.sum(values * values, axis=1, keepdims=True) + NORM_EPS)
        emb[t, rows, :] = (values * inverse).astype(jnp.bfloat16)
        row_info[rows, t : t + 1] = inverse

    for way in range(2):
        ring(way, 0).start()
    for way in range(2):
        ring(way, 1).start()
    for t in range(2):
        sib(t, -1).start()
    for o, r in partners:
        label_copy(o, r).start()

    @pl.when(core == 0)
    def _():
        err_copy(1).start()
        err_local(0).start()

    @pl.when(core == 1)
    def _():
        err_copy(0).start()
        err_local(1).start()

    lab[0, 0] = labels[...]
    row_sum[...] = jnp.zeros_like(row_sum)
    col_sum[...] = jnp.zeros_like(col_sum)
    for t in range(2):
        normalize(0, 0, t)
    for t, hidden in enumerate((hidden_a, hidden_b)):
        for k in range(n_z):
            stage[t, k] = hidden[:, k * feat : (k + 1) * feat]

    tile = 256

    def tile_logits(r0, c0):
        x = emb[core, pl.ds(r0, tile), :]
        y = emb[other, pl.ds(c0, tile), :]
        part = jnp.exp(
            logit_scale * lax.dot_general(x, y, NT, preferred_element_type=jnp.float32)
        )
        logit[pl.ds(r0, tile), pl.ds(c0, tile)] = part
        lanes = part[:, 0:128]
        for k in range(1, tile // 128):
            lanes = lanes + part[:, k * 128 : (k + 1) * 128]
        row_sum[pl.ds(r0, tile), :] += lanes
        col_sum[:, pl.ds(c0, tile)] += jnp.sum(part.reshape(tile // 8, 8, tile), axis=0)

    def logits_to(old, new):
        def columns(k, _):
            c0 = pl.multiple_of(old + (k // (new // tile)) * tile, tile)
            r0 = pl.multiple_of(lax.rem(k, new // tile) * tile, tile)
            tile_logits(r0, c0)
            return 0

        lax.fori_loop(0, ((new - old) // tile) * (new // tile), columns, 0)
        if old:

            def rows(k, _):
                c0 = pl.multiple_of((k // ((new - old) // tile)) * tile, tile)
                r0 = pl.multiple_of(old + lax.rem(k, (new - old) // tile) * tile, tile)
                tile_logits(r0, c0)
                return 0

            lax.fori_loop(0, ((new - old) // tile) * (old // tile), rows, 0)

    last = len(RING[0])
    bounds = [chip * k // tile * tile for k in (3, 5, 7)]
    done = 0
    for n in range(last):
        for way in range(2):
            ring(way, n).wait_recv()
            if n + 2 < last:
                ring(way, n + 2).start()
            sib(way, n).start()
        for way in range(2):
            dist, t = RING[way][n]
            normalize(SLOT_OF[dist] if way == 0 else SLOT_OF[n_z - dist], 0, t)
            sib(way, n - 1).wait_recv()
            if n == 0:
                normalize(0, 1, way)
            else:
                dist, t = RING[way][n - 1]
                normalize(SLOT_OF[dist] if way == 0 else SLOT_OF[n_z - dist], 1, t)
        if n == last - 1:
            for o, r in partners:
                hidden_copy(o, r).start()
        if n in (2, 4, 6):
            logits_to(done, bounds[n // 2 - 1])
            done = bounds[n // 2 - 1]
    for way in range(2):
        sib(way, last - 1).wait_recv()
        dist, t = RING[way][last - 1]
        normalize(SLOT_OF[dist] if way == 0 else SLOT_OF[n_z - dist], 1, t)

    for o, r in partners:
        label_copy(o, r).wait_recv()
    for slot in range(n_z):
        where = lax.rem(z + n_z - BEHIND[slot], n_z)
        for r in range(2):
            first = ((where * 2 + (other if r else core)) * tok).astype(jnp.float32)
            piece = lab[slot, r]
            spread = jnp.broadcast_to(piece[0:1, :], (128, piece.shape[1])).T[:tok, 0:1]
            own = first + lax.broadcasted_iota(jnp.int32, (tok, 1), 0).astype(jnp.float32)
            rows = pl.ds(slot * chip + r * tok, tok)
            row_info[rows, 2:3] = jnp.where(core == 0, spread, own)
            row_info[rows, 3:4] = jnp.where(core == 0, own, spread)
    for k in range(group // 128):
        ids = row_info[k * 128 : (k + 1) * 128, 3:4]
        col_id[:, k * 128 : (k + 1) * 128] = jnp.broadcast_to(ids, (128, 128)).T[0:8, :]

    logits_to(done, group)

    row_info[:, 4:5] = 0.5 / jnp.sum(row_sum[...], axis=1, keepdims=True)
    col_sum[0:1, :] = 0.5 / jnp.sum(col_sum[...], axis=0, keepdims=True)
    row_info[:, 5:6] = jnp.where(core == 0, row_info[:, 0:1], row_info[:, 1:2])

    chunk = weight.shape[0]
    fine = 16

    def chunk_step(k, _):
        r0 = pl.multiple_of(k * chunk, chunk)

        def weights(m, _):
            rows = pl.ds(pl.multiple_of(r0 + m * fine, fine), fine)
            base = row_info[rows, 4:5]
            ids = row_info[rows, 2:3]
            value = logit[rows, :] * (base + col_sum[0:1, :])
            value = value - jnp.where(ids == col_id[0:1, :], 1.0, 0.0)
            weight[pl.ds(pl.multiple_of(m * fine, fine), fine), :] = value.astype(jnp.bfloat16)
            return 0

        lax.fori_loop(0, chunk // fine, weights, 0)
        grad[...] = lax.dot_general(
            weight[...], emb[other], NN, preferred_element_type=jnp.float32
        )

        def finish(m, _):
            rows = pl.ds(pl.multiple_of(r0 + m * fine, fine), fine)
            inverse = row_info[rows, 5:6]
            unit = raw[core, rows, :].astype(jnp.float32) * inverse
            value = logit_scale * grad[pl.ds(pl.multiple_of(m * fine, fine), fine), :]
            along = jnp.sum(unit * value, axis=1, keepdims=True)
            emb[core, rows, :] = ((value - unit * along) * inverse).astype(jnp.bfloat16)
            return 0

        lax.fori_loop(0, chunk // fine, finish, 0)
        return 0

    lax.fori_loop(0, group // chunk, chunk_step, 0)

    hid[0:tok, :] = stage[core, z]
    for o, r in partners:
        hidden_copy(o, r).wait_recv()
    err_copy(0).wait_recv()
    err_local(0).wait()
    total = lax.dot_general(hid[...], emb[core], TN, preferred_element_type=jnp.float32)
    for k in range(2):
        rows = slice(k * slab, (k + 1) * slab)
        mem_ref[rows, :] = total[rows, :] + err[jnp.where(core == k, 0, 1)]

    for way in range(2):
        for n in range(last):
            ring(way, n).wait_send()
            sib(way, n).wait_send()
        sib(way, -1).wait_send()
    for o, r in partners:
        label_copy(o, r).wait_send()
        hidden_copy(o, r).wait_send()
    err_copy(0).wait_send()


def head_gradient(n_z, proj_a, proj_b, labels, hidden_a, hidden_b, err_a, err_b):
    tok, width = proj_a.shape
    group = tok * n_z * 2
    feat = hidden_a.shape[1] // n_z
    slab = err_a.shape[1]
    wide = labels.shape[1]
    chunk = 256
    dma = pltpu.SemaphoreType.DMA
    any_space = pl.BlockSpec(memory_space=pl.ANY)
    vmem = pl.BlockSpec(memory_space=pltpu.VMEM)
    return pl.pallas_call(
        functools.partial(grads_kernel, n_z),
        out_shape=jax.ShapeDtypeStruct((feat, width), jnp.float32),
        in_specs=[any_space, any_space, vmem, vmem, vmem, any_space, any_space],
        out_specs=vmem,
        scratch_shapes=[
            pltpu.VMEM((2, group, width), jnp.bfloat16),
            pltpu.VMEM((2, group, width), jnp.bfloat16),
            pltpu.VMEM((group, group), jnp.float32),
            pltpu.VMEM((chunk, group), jnp.bfloat16),
            pltpu.VMEM((chunk, width), jnp.float32),
            pltpu.VMEM((group, 128), jnp.float32),
            pltpu.VMEM((8, group), jnp.float32),
            pltpu.VMEM((group, 128), jnp.float32),
            pltpu.VMEM((8, group), jnp.float32),
            pltpu.VMEM((n_z, 2, 8, wide), jnp.float32),
            pltpu.VMEM((2, n_z, tok, feat), jnp.bfloat16),
            pltpu.VMEM((group, feat), jnp.bfloat16),
            pltpu.VMEM((2, slab, width), jnp.float32),
            dma((2, 7)),
            dma((2, 7)),
            dma((2, 8)),
            dma((2, 8)),
            dma((n_z, 2)),
            dma((n_z, 2)),
            dma((n_z, 2)),
            dma((n_z, 2)),
            dma,
            dma,
            dma((3,)),
        ],
        compiler_params=pltpu.CompilerParams(
            collective_id=0, has_side_effects=True, vmem_limit_bytes=63 * 1024 * 1024
        ),
        name="head_gradient",
    )(proj_a, proj_b, labels, hidden_a, hidden_b, err_a, err_b)


def compress_kernel(
    n_y, n_x, n_z, mem, seed,
    p_ref, q_ref, new_ref,
    mem_sib, x_buf, y_buf, g_buf, part, gathered, z_buf, full, state, basis, q_own, q_sib, p_own, p_sib,
    x_send, x_recv, y_send, y_recv, g_send, g_recv, r_send, r_recv, z_send, z_recv,
    f_send, f_recv, sib_send, sib_recv,
):
    n_rep = n_y * n_x
    slab = mem_sib.shape[0]
    rank = seed.shape[1]
    width = mem.shape[1]
    rep = lax.axis_index("rep")
    con = lax.axis_index("con")
    y = rep // n_x
    x = lax.rem(rep, n_x)
    z = con // 2
    core = lax.rem(con, 2)
    other = 1 - core
    sibling = (rep, z * 2 + other)

    def along_x(i):
        return (y * n_x + lax.rem(x + i, n_x), con)

    def along_y(i):
        return (lax.rem(y + i, n_y) * n_x + x, con)

    def along_z(i):
        return (rep, lax.rem(z + i, n_z) * 2 + core)

    def along_rep(i):
        return (lax.rem(rep + i, n_rep), con)

    barrier = pltpu.get_barrier_semaphore()
    greet = [along_rep(i) for i in range(1, n_rep)] + [along_z(i) for i in range(1, n_z)]
    for peer in greet + [sibling]:
        pl.semaphore_signal(barrier, inc=1, device_id=peer, device_id_type=MESH)
    pl.semaphore_wait(barrier, len(greet) + 1)

    def copy(source, target, send, recv, peer):
        return pltpu.make_async_remote_copy(
            src_ref=source, dst_ref=target, send_sem=send, recv_sem=recv,
            device_id=peer, device_id_type=MESH,
        )

    theirs = pl.ds(pl.multiple_of(other * slab, 8), slab)
    ours = pl.ds(pl.multiple_of(core * slab, 8), slab)
    mem_copy = copy(mem.at[theirs, :], mem_sib, sib_send.at[0], sib_recv.at[0], sibling)
    mem_copy.start()

    def all_sum(buf, index, count, send, recv, peers, value):
        buf[index] = value
        copies = [
            copy(buf.at[index], buf.at[index], send.at[i], recv.at[i], peers(i))
            for i in range(1, count)
        ]
        for one in copies:
            one.start()

        def finish():
            for one in copies:
                one.wait()
            total = buf[0]
            for k in range(1, count):
                total = total + buf[k]
            return total

        return finish

    left = exact(mem[...], seed[...], NN)
    packed = jnp.concatenate([left[:slab, :], left[slab:, :]], axis=1)
    packed = all_sum(x_buf, x, n_x, x_send, x_recv, along_x, packed)()
    packed = all_sum(y_buf, y, n_y, y_send, y_recv, along_y, packed)()
    left = jnp.concatenate([packed[:, :rank], packed[:, rank:]], axis=0)

    gram = exact(left, left, TN)
    gram_sum = all_sum(
        g_buf, z, n_z, g_send, g_recv, along_z,
        jnp.concatenate([gram[: rank // 2, :], gram[rank // 2 :, :]], axis=1),
    )
    right = exact(left, mem[...], TN)
    span = width // 2
    for k in range(n_rep):
        part[k] = right[8 * (k // 2) : 8 * (k // 2) + 8, span * (k % 2) : span * (k % 2) + span]
    gathered[rep] = part[rep]
    reduce = [
        copy(
            part.at[lax.rem(rep + i, n_rep)], gathered.at[rep], r_send.at[i], r_recv.at[i],
            along_rep(i),
        )
        for i in range(1, n_rep)
    ]
    for one in reduce:
        one.start()

    gram = gram_sum()
    gram = jnp.concatenate([gram[:, :rank], gram[:, rank:]], axis=0)
    eye = (
        lax.broadcasted_iota(jnp.int32, (rank, rank), 0)
        == lax.broadcasted_iota(jnp.int32, (rank, rank), 1)
    ).astype(jnp.float32)
    state[...] = jnp.concatenate([eye, gram], axis=1)

    def column_step(k, _):
        value = state[...]
        row = state[pl.ds(k, 1), :]
        lane_row = lax.broadcasted_iota(jnp.int32, (1, 2 * rank), 1)
        lane = lax.broadcasted_iota(jnp.int32, (rank, 2 * rank), 1)
        product = jnp.where(lane_row < rank, row * pltpu.roll(row, rank, 1), 0.0)
        square = jnp.maximum(jnp.sum(product, axis=1, keepdims=True), 0.0) + NORM_EPS
        column = jnp.sum(jnp.where(lane == rank + k, value, 0.0), axis=1, keepdims=True)
        basis[pl.ds(k, 1), :] = row * lax.rsqrt(square)
        state[...] = value - column * (row / square)
        return 0

    cuts = [0, rank // 3, 2 * rank // 3, rank]
    lax.fori_loop(cuts[0], cuts[1], column_step, 0)
    for one in reduce:
        one.wait()
    total = gathered[0]
    for k in range(1, n_rep):
        total = total + gathered[k]
    z_sum = all_sum(z_buf, z, n_z, z_send, z_recv, along_z, total)
    lax.fori_loop(cuts[1], cuts[2], column_step, 0)
    full[rep] = z_sum()
    spread = [
        copy(full.at[rep], full.at[rep], f_send.at[i], f_recv.at[i], along_rep(i))
        for i in range(1, n_rep)
    ]
    for one in spread:
        one.start()
    lax.fori_loop(cuts[2], cuts[3], column_step, 0)

    turn = basis[:, :rank]
    p_own[...] = exact(left, turn, NT)
    p_copy = copy(p_own.at[theirs, :], p_sib, sib_send.at[1], sib_recv.at[1], sibling)
    p_copy.start()
    for one in spread:
        one.wait()
    right = jnp.concatenate(
        [jnp.concatenate([full[2 * k], full[2 * k + 1]], axis=1) for k in range(n_rep // 2)],
        axis=0,
    )
    q_own[...] = exact(turn, right, NN) / n_rep
    q_copy = copy(q_own, q_sib, sib_send.at[2], sib_recv.at[2], sibling)
    q_copy.start()
    new_ref[core] = mem[ours, :] - exact(p_own[ours, :], q_own[...], NN)
    p_ref[core] = p_own[ours, :]
    q_ref[core] = q_own[...].T
    mem_copy.wait()
    p_copy.wait()
    q_copy.wait()
    new_ref[other] = mem_sib[...] - exact(p_sib[...], q_sib[...], NN)
    p_ref[other] = p_sib[...]
    q_ref[other] = q_sib[...].T


def compress(n_y, n_x, n_z, mem, seed):
    feat, width = mem.shape
    rank = seed.shape[1]
    slab = feat // 2
    n_rep = n_y * n_x
    dma = pltpu.SemaphoreType.DMA
    vmem = pl.BlockSpec(memory_space=pltpu.VMEM)
    f32 = jnp.float32
    return pl.pallas_call(
        functools.partial(compress_kernel, n_y, n_x, n_z),
        out_shape=(
            jax.ShapeDtypeStruct((2, slab, rank), f32),
            jax.ShapeDtypeStruct((2, width, rank), f32),
            jax.ShapeDtypeStruct((2, slab, width), f32),
        ),
        in_specs=[vmem] * 2,
        out_specs=[vmem] * 3,
        scratch_shapes=[
            pltpu.VMEM((slab, width), f32),
            pltpu.VMEM((n_x, slab, 2 * rank), f32),
            pltpu.VMEM((n_y, slab, 2 * rank), f32),
            pltpu.VMEM((n_z, rank // 2, 2 * rank), f32),
            pltpu.VMEM((n_rep, 8, width // 2), f32),
            pltpu.VMEM((n_rep, 8, width // 2), f32),
            pltpu.VMEM((n_z, 8, width // 2), f32),
            pltpu.VMEM((n_rep, 8, width // 2), f32),
            pltpu.VMEM((rank, 2 * rank), f32),
            pltpu.VMEM((rank, 2 * rank), f32),
            pltpu.VMEM((rank, width), f32),
            pltpu.VMEM((rank, width), f32),
            pltpu.VMEM((feat, rank), f32),
            pltpu.VMEM((slab, rank), f32),
            dma((n_x,)), dma((n_x,)),
            dma((n_y,)), dma((n_y,)),
            dma((n_z,)), dma((n_z,)),
            dma((n_rep,)), dma((n_rep,)),
            dma((n_z,)), dma((n_z,)),
            dma((n_rep,)), dma((n_rep,)),
            dma((3,)), dma((3,)),
        ],
        compiler_params=pltpu.CompilerParams(
            collective_id=1, has_side_effects=True, vmem_limit_bytes=32 * 1024 * 1024
        ),
        name="compress",
    )(mem, seed)


def shards(
    audio_hidden, score_hidden, audio_proj, score_proj, labels, q_seed, err_audio, err_score
):
    n_z = 8
    n_y = n_x = 4
    tok = labels.shape[1]
    wide = -(-tok // 128) * 128
    spread = jnp.pad(labels.astype(jnp.float32), ((0, 7), (0, wide - tok)))
    mem = head_gradient(
        n_z, audio_proj, score_proj, spread, audio_hidden, score_hidden, err_audio, err_score
    )
    p, q, new = compress(n_y, n_x, n_z, mem, q_seed)
    return (p[0], q[0], new[0:1], p[1], q[1], new[1:2])


def solution(mesh):
    placed = (
        P(("rep", "con"), None),
        P(("rep", "con"), None),
        P(("rep", "con"), None),
        P(("rep", "con"), None),
        P("rep", "con"),
        P(),
        P("rep", "con", None),
        P("rep", "con", None),
    )
    return jax.shard_map(
        shards,
        mesh=mesh,
        in_specs=placed,
        out_specs=(
            P("con", None),
            P(),
            P("rep", "con", None),
            P("con", None),
            P(),
            P("rep", "con", None),
        ),
        check_vma=False,
    )
```

```python
import functools

import jax
import jax.numpy as jnp
from jax import lax
from jax.experimental import pallas as pl
from jax.experimental.pallas import tpu as pltpu
from jax.sharding import PartitionSpec as P

MESH = pl.DeviceIdType.MESH
logit_scale = 30.0
NORM_EPS = 1e-06
LOG2E = 1.4426950408889634
NT = (((1,), (1,)), ((), ()))
TN = (((0,), (0,)), ((), ()))
NN = (((1,), (0,)), ((), ()))
HIGH = lax.Precision.HIGHEST

SLOT_OF = (0, 1, 3, 5, 7, 6, 4, 2)
BEHIND = (0, 1, 7, 2, 6, 3, 5, 4)
RING = (
    ((1, 0), (1, 1), (2, 0), (2, 1), (3, 0), (3, 1), (4, 0)),
    ((1, 1), (1, 0), (2, 1), (2, 0), (3, 1), (3, 0), (4, 1)),
)


def exact(left, right, dims):
    return lax.dot_general(
        left, right, dims, precision=HIGH, preferred_element_type=jnp.float32
    )


def grads_kernel(
    n_z, proj_a, proj_b, labels, hidden_a, hidden_b, err_a, err_b,
    mem_ref,
    raw, emb, logit, weight, grad, row_sum, col_sum, row_info, col_id, lab, pair, stage, blocks,
    hid, err,
    ring_send, ring_recv, sib_send, sib_recv, lab_send, lab_recv, hid_send, hid_recv,
    near_send, near_recv, local_sem,
):
    tok = proj_a.shape[0]
    chip = 2 * tok
    group = raw.shape[1]
    feat = hid.shape[1]
    slab = err_a.shape[1]
    rep = lax.axis_index("rep")
    con = lax.axis_index("con")
    z = con // 2
    core = lax.rem(con, 2)
    other = 1 - core

    def plane(ahead):
        return (rep, lax.rem(z + ahead, n_z) * 2 + core)

    sibling = (rep, z * 2 + other)

    projs = (proj_a, proj_b)
    loads = [
        pltpu.make_async_copy(projs[t], raw.at[t, pl.ds(0, tok), :], local_sem.at[t])
        for t in range(2)
    ]
    for load in loads:
        load.start()

    barrier = pltpu.get_barrier_semaphore()
    for peer in (plane(1), plane(n_z - 1), sibling):
        pl.semaphore_signal(barrier, inc=1, device_id=peer, device_id_type=MESH)
    pl.semaphore_wait(barrier, 3)
    for load in loads:
        load.wait()

    def remote(source, target, send, recv, peer):
        return pltpu.make_async_remote_copy(
            src_ref=source, dst_ref=target, send_sem=send, recv_sem=recv,
            device_id=peer, device_id_type=MESH,
        )

    def slot_at(way, dist):
        return SLOT_OF[dist] if way == 0 else SLOT_OF[(n_z - dist) % n_z]

    def ring(way, n):
        dist, t = RING[way][n]
        return remote(
            raw.at[t, pl.ds(slot_at(way, dist - 1) * chip, tok), :],
            raw.at[t, pl.ds(slot_at(way, dist) * chip, tok), :],
            ring_send.at[way, n],
            ring_recv.at[way, n],
            plane(1 if way == 0 else n_z - 1),
        )

    def sib(way, n):
        dist, t = RING[way][n] if n < 7 else (0, way)
        rows = slot_at(way, dist) * chip
        return remote(
            raw.at[t, pl.ds(rows, tok), :],
            raw.at[t, pl.ds(rows + tok, tok), :],
            sib_send.at[way, n],
            sib_recv.at[way, n],
            sibling,
        )

    def lab_copy(o):
        return remote(
            lab.at[0], lab.at[SLOT_OF[o]], lab_send.at[o], lab_recv.at[o], plane(o)
        )

    def hid_copy(o):
        return remote(
            stage.at[lax.rem(z + o, n_z)], blocks.at[SLOT_OF[o]],
            hid_send.at[o], hid_recv.at[o], plane(o),
        )

    def lab_near():
        return remote(lab.at[0, 0], lab.at[0, 1], near_send.at[0], near_recv.at[0], sibling)

    def hid_near(source):
        return remote(source, pair.at[1], near_send.at[1], near_recv.at[1], sibling)

    def err_near(source):
        return remote(source.at[0], err.at[1], near_send.at[2], near_recv.at[2], sibling)

    def hid_local(source):
        return pltpu.make_async_copy(source, pair.at[0], local_sem.at[2])

    def err_local(source):
        return pltpu.make_async_copy(source.at[0], err.at[0], local_sem.at[3])

    def normalize(slot, cross, t):
        rows = pl.ds(slot * chip + cross * tok, tok)
        values = raw[t, rows, :].astype(jnp.float32)
        inverse = lax.rsqrt(jnp.sum(values * values, axis=1, keepdims=True) + NORM_EPS)
        emb[t, rows, :] = (values * inverse).astype(jnp.bfloat16)
        row_info[rows, t : t + 1] = inverse

    for n in range(2):
        for way in range(2):
            ring(way, n).start()
    for t in range(2):
        sib(t, 7).start()
    lab[0, 0] = jnp.zeros(lab.shape[2:], jnp.float32)
    lab[0, 0, :, 0:tok] = jnp.broadcast_to(labels[...].astype(jnp.float32), (8, tok))
    lab_near().start()

    @pl.when(core == 0)
    def _():
        hid_near(hidden_b).start()
        hid_local(hidden_a).start()
        err_near(err_b).start()
        err_local(err_a).start()

    @pl.when(core == 1)
    def _():
        hid_near(hidden_a).start()
        hid_local(hidden_b).start()
        err_near(err_a).start()
        err_local(err_b).start()

    row_sum[...] = jnp.zeros_like(row_sum)
    col_sum[...] = jnp.zeros_like(col_sum)
    for t in range(2):
        normalize(0, 0, t)
    for t in range(2):
        sib(t, 7).wait_recv()
        normalize(0, 1, t)

    def tile_logits(r0, c0, size):
        x = emb[core, pl.ds(r0, size), :]
        y = emb[other, pl.ds(c0, size), :]
        part = jnp.exp2(
            (logit_scale * LOG2E) * lax.dot_general(x, y, NT, preferred_element_type=jnp.float32)
        )
        logit[pl.ds(r0, size), pl.ds(c0, size)] = part
        lanes = part[:, 0:128]
        for k in range(1, size // 128):
            lanes = lanes + part[:, k * 128 : (k + 1) * 128]
        row_sum[pl.ds(r0, size), :] += lanes
        col_sum[:, pl.ds(c0, size)] += jnp.sum(part.reshape(size // 8, 8, size), axis=0)

    def logits_to(old, new):
        size = new - old

        def columns(k, _):
            tile_logits(pl.multiple_of(k * size, 256), old, size)
            return 0

        def rows(k, _):
            tile_logits(old, pl.multiple_of(k * size, 256), size)
            return 0

        lax.fori_loop(0, new // size, columns, 0)
        if old:
            lax.fori_loop(0, old // size, rows, 0)

    wide = stage.shape[2]
    narrow = feat - wide
    part_rows = chip * narrow // wide

    def pack():
        for half in range(2):
            for k in range(n_z):
                first = k * feat
                stage[k, half * tok : (half + 1) * tok, :] = pair[half, :, first : first + wide]
                for g in range(tok // part_rows):
                    lane = (half * (tok // part_rows) + g) * narrow
                    stage[k, chip : chip + part_rows, lane : lane + narrow] = pair[
                        half, g * part_rows : (g + 1) * part_rows, first + wide : first + feat
                    ]

    def unpack(slot, block):
        rows = slot * chip
        hid[rows : rows + chip, 0:wide] = block[0:chip, :]
        for g in range(chip // part_rows):
            hid[rows + g * part_rows : rows + (g + 1) * part_rows, wide:feat] = block[
                chip : chip + part_rows, g * narrow : (g + 1) * narrow
            ]

    last = len(RING[0])
    bounds = (0, 768, 1536, 2048, group)
    for n in range(last):
        for way in range(2):
            ring(way, n).wait_recv()
            if n + 2 < last:
                ring(way, n + 2).start()
            sib(way, n).start()
        if n == last - 1:
            for o in range(1, n_z):
                lab_copy(o).start()
            for o in range(1, n_z):
                hid_copy(o).start()
        for way in range(2):
            dist, t = RING[way][n]
            normalize(slot_at(way, dist), 0, t)
        if n == 0:
            hid_near(hidden_a).wait_recv()
            hid_local(hidden_a).wait()
            pack()
            lab_near().wait_recv()
        for way in range(2):
            dist, t = RING[way][n]
            sib(way, n).wait_recv()
            normalize(slot_at(way, dist), 1, t)
        if n % 2:
            logits_to(bounds[n // 2], bounds[n // 2 + 1])
    logits_to(bounds[3], bounds[4])

    for o in range(1, n_z):
        lab_copy(o).wait_recv()
    for slot in range(n_z):
        where = lax.rem(z + n_z - BEHIND[slot], n_z)
        for r in range(2):
            first = ((where * 2 + (other if r else core)) * tok).astype(jnp.float32)
            piece = lab[slot, r]
            spread = jnp.broadcast_to(piece[0:1, :], (128, piece.shape[1])).T[:tok, 0:1]
            own = first + lax.broadcasted_iota(jnp.int32, (tok, 1), 0).astype(jnp.float32)
            rows = pl.ds(slot * chip + r * tok, tok)
            row_info[rows, 2:3] = jnp.where(core == 0, spread, own)
            row_info[rows, 3:4] = jnp.where(core == 0, own, spread)
    for k in range(group // 128):
        ids = row_info[k * 128 : (k + 1) * 128, 3:4]
        col_id[:, k * 128 : (k + 1) * 128] = jnp.broadcast_to(ids, (128, 128)).T[0:8, :]

    row_info[:, 4:5] = 0.5 / jnp.sum(row_sum[...], axis=1, keepdims=True)
    col_sum[0:1, :] = 0.5 / jnp.sum(col_sum[...], axis=0, keepdims=True)
    row_info[:, 5:6] = jnp.where(core == 0, row_info[:, 0:1], row_info[:, 1:2])

    chunk = weight.shape[0]
    fine = 16

    def chunk_step(k, _):
        r0 = pl.multiple_of(k * chunk, chunk)
        for m in range(chunk // fine):
            rows = pl.ds(r0 + m * fine, fine)
            value = logit[rows, :] * (row_info[rows, 4:5] + col_sum[0:1, :])
            value = value - jnp.where(row_info[rows, 2:3] == col_id[0:1, :], 1.0, 0.0)
            weight[m * fine : (m + 1) * fine, :] = value.astype(jnp.bfloat16)
        grad[...] = lax.dot_general(
            weight[...], emb[other], NN, preferred_element_type=jnp.float32
        )
        for m in range(chunk // fine):
            rows = pl.ds(r0 + m * fine, fine)
            inverse = row_info[rows, 5:6]
            unit = raw[core, rows, :].astype(jnp.float32) * inverse
            value = logit_scale * grad[m * fine : (m + 1) * fine, :]
            along = jnp.sum(unit * value, axis=1, keepdims=True)
            emb[core, rows, :] = ((value - unit * along) * inverse).astype(jnp.bfloat16)
        return 0

    lax.fori_loop(0, group // chunk, chunk_step, 0)

    unpack(0, stage.at[z])
    for o in range(1, n_z):
        hid_copy(o).wait_recv()
        unpack(SLOT_OF[o], blocks.at[SLOT_OF[o]])
    err_near(err_a).wait_recv()
    err_local(err_a).wait()
    total = lax.dot_general(hid[...], emb[core], TN, preferred_element_type=jnp.float32)
    for k in range(2):
        rows = slice(k * slab, (k + 1) * slab)
        mem_ref[rows, :] = total[rows, :] + err[jnp.where(core == k, 0, 1)]

    for way in range(2):
        for n in range(last):
            ring(way, n).wait_send()
        for n in range(last + 1):
            sib(way, n).wait_send()
    for o in range(1, n_z):
        lab_copy(o).wait_send()
        hid_copy(o).wait_send()
    lab_near().wait_send()
    hid_near(hidden_a).wait_send()
    err_near(err_a).wait_send()


def head_gradient(n_z, proj_a, proj_b, labels, hidden_a, hidden_b, err_a, err_b):
    tok, width = proj_a.shape
    group = tok * n_z * 2
    feat = hidden_a.shape[1] // n_z
    slab = err_a.shape[1]
    chunk = 256
    packed = 2 * tok * feat // 128
    dma = pltpu.SemaphoreType.DMA
    any_space = pl.BlockSpec(memory_space=pl.ANY)
    vmem = pl.BlockSpec(memory_space=pltpu.VMEM)
    return pl.pallas_call(
        functools.partial(grads_kernel, n_z),
        out_shape=jax.ShapeDtypeStruct((feat, width), jnp.float32),
        in_specs=[any_space, any_space, vmem] + [any_space] * 4,
        out_specs=vmem,
        scratch_shapes=[
            pltpu.VMEM((2, group, width), jnp.bfloat16),
            pltpu.VMEM((2, group, width), jnp.bfloat16),
            pltpu.VMEM((group, group), jnp.float32),
            pltpu.VMEM((chunk, group), jnp.bfloat16),
            pltpu.VMEM((chunk, width), jnp.float32),
            pltpu.VMEM((group, 128), jnp.float32),
            pltpu.VMEM((8, group), jnp.float32),
            pltpu.VMEM((group, 128), jnp.float32),
            pltpu.VMEM((8, group), jnp.float32),
            pltpu.VMEM((n_z, 2, 8, 256), jnp.float32),
            pltpu.VMEM((2, tok, feat * n_z), jnp.bfloat16),
            pltpu.VMEM((n_z, packed, 128), jnp.bfloat16),
            pltpu.VMEM((n_z, packed, 128), jnp.bfloat16),
            pltpu.VMEM((group, feat), jnp.bfloat16),
            pltpu.VMEM((2, slab, width), jnp.float32),
            dma((2, 7)),
            dma((2, 7)),
            dma((2, 8)),
            dma((2, 8)),
            dma((n_z,)),
            dma((n_z,)),
            dma((n_z,)),
            dma((n_z,)),
            dma((3,)),
            dma((3,)),
            dma((4,)),
        ],
        compiler_params=pltpu.CompilerParams(
            collective_id=0, has_side_effects=True, vmem_limit_bytes=63 * 1024 * 1024
        ),
        name="head_gradient",
    )(proj_a, proj_b, labels, hidden_a, hidden_b, err_a, err_b)


def compress_kernel(
    n_y, n_x, n_z, mem, seed,
    p_ref, q_ref, new_ref,
    mem_sib, x_buf, y_buf, g_buf, part, gathered, z_buf, full, state, basis, q_own, q_sib, p_own, p_sib,
    x_send, x_recv, y_send, y_recv, g_send, g_recv, r_send, r_recv, z_send, z_recv,
    f_send, f_recv, sib_send, sib_recv,
):
    n_rep = n_y * n_x
    slab = mem_sib.shape[0]
    rank = seed.shape[1]
    width = mem.shape[1]
    rep = lax.axis_index("rep")
    con = lax.axis_index("con")
    y = rep // n_x
    x = lax.rem(rep, n_x)
    z = con // 2
    core = lax.rem(con, 2)
    other = 1 - core
    sibling = (rep, z * 2 + other)

    def along_x(i):
        return (y * n_x + lax.rem(x + i, n_x), con)

    def along_y(i):
        return (lax.rem(y + i, n_y) * n_x + x, con)

    def along_z(i):
        return (rep, lax.rem(z + i, n_z) * 2 + core)

    def along_rep(i):
        return (lax.rem(rep + i, n_rep), con)

    barrier = pltpu.get_barrier_semaphore()
    greet = [along_rep(i) for i in range(1, n_rep)] + [along_z(i) for i in range(1, n_z)]
    for peer in greet + [sibling]:
        pl.semaphore_signal(barrier, inc=1, device_id=peer, device_id_type=MESH)
    pl.semaphore_wait(barrier, len(greet) + 1)

    def copy(source, target, send, recv, peer):
        return pltpu.make_async_remote_copy(
            src_ref=source, dst_ref=target, send_sem=send, recv_sem=recv,
            device_id=peer, device_id_type=MESH,
        )

    theirs = pl.ds(pl.multiple_of(other * slab, 8), slab)
    ours = pl.ds(pl.multiple_of(core * slab, 8), slab)
    mem_copy = copy(mem.at[theirs, :], mem_sib, sib_send.at[0], sib_recv.at[0], sibling)
    mem_copy.start()

    def all_sum(buf, index, count, send, recv, peers, value):
        buf[index] = value
        copies = [
            copy(buf.at[index], buf.at[index], send.at[i], recv.at[i], peers(i))
            for i in range(1, count)
        ]
        for one in copies:
            one.start()

        def finish():
            for one in copies:
                one.wait()
            total = buf[0]
            for k in range(1, count):
                total = total + buf[k]
            return total

        return finish

    left = exact(mem[...], seed[...], NN)
    packed = jnp.concatenate([left[:slab, :], left[slab:, :]], axis=1)
    packed = all_sum(x_buf, x, n_x, x_send, x_recv, along_x, packed)()
    packed = all_sum(y_buf, y, n_y, y_send, y_recv, along_y, packed)()
    left = jnp.concatenate([packed[:, :rank], packed[:, rank:]], axis=0)

    gram = exact(left, left, TN)
    gram_sum = all_sum(
        g_buf, z, n_z, g_send, g_recv, along_z,
        jnp.concatenate([gram[: rank // 2, :], gram[rank // 2 :, :]], axis=1),
    )
    right = exact(left, mem[...], TN)
    span = width // 2
    for k in range(n_rep):
        part[k] = right[8 * (k // 2) : 8 * (k // 2) + 8, span * (k % 2) : span * (k % 2) + span]
    gathered[rep] = part[rep]
    reduce = [
        copy(
            part.at[lax.rem(rep + i, n_rep)], gathered.at[rep], r_send.at[i], r_recv.at[i],
            along_rep(i),
        )
        for i in range(1, n_rep)
    ]
    for one in reduce:
        one.start()

    gram = gram_sum()
    gram = jnp.concatenate([gram[:, :rank], gram[:, rank:]], axis=0)
    eye = (
        lax.broadcasted_iota(jnp.int32, (rank, rank), 0)
        == lax.broadcasted_iota(jnp.int32, (rank, rank), 1)
    ).astype(jnp.float32)
    state[...] = jnp.concatenate([eye, gram], axis=1)

    def column_step(k, _):
        value = state[...]
        row = state[pl.ds(k, 1), :]
        lane_row = lax.broadcasted_iota(jnp.int32, (1, 2 * rank), 1)
        lane = lax.broadcasted_iota(jnp.int32, (rank, 2 * rank), 1)
        product = jnp.where(lane_row < rank, row * pltpu.roll(row, rank, 1), 0.0)
        square = jnp.maximum(jnp.sum(product, axis=1, keepdims=True), 0.0) + NORM_EPS
        column = jnp.sum(jnp.where(lane == rank + k, value, 0.0), axis=1, keepdims=True)
        basis[pl.ds(k, 1), :] = row * lax.rsqrt(square)
        state[...] = value - column * (row / square)
        return 0

    cuts = [0, rank // 3, 2 * rank // 3, rank]
    lax.fori_loop(cuts[0], cuts[1], column_step, 0)
    for one in reduce:
        one.wait()
    total = gathered[0]
    for k in range(1, n_rep):
        total = total + gathered[k]
    z_sum = all_sum(z_buf, z, n_z, z_send, z_recv, along_z, total)
    lax.fori_loop(cuts[1], cuts[2], column_step, 0)
    full[rep] = z_sum()
    spread = [
        copy(full.at[rep], full.at[rep], f_send.at[i], f_recv.at[i], along_rep(i))
        for i in range(1, n_rep)
    ]
    for one in spread:
        one.start()
    lax.fori_loop(cuts[2], cuts[3], column_step, 0)

    turn = basis[:, :rank]
    p_own[...] = exact(left, turn, NT)
    p_copy = copy(p_own.at[theirs, :], p_sib, sib_send.at[1], sib_recv.at[1], sibling)
    p_copy.start()
    for one in spread:
        one.wait()
    right = jnp.concatenate(
        [jnp.concatenate([full[2 * k], full[2 * k + 1]], axis=1) for k in range(n_rep // 2)],
        axis=0,
    )
    q_own[...] = exact(turn, right, NN) / n_rep
    q_copy = copy(q_own, q_sib, sib_send.at[2], sib_recv.at[2], sibling)
    q_copy.start()
    new_ref[core] = mem[ours, :] - exact(p_own[ours, :], q_own[...], NN)
    p_ref[core] = p_own[ours, :]
    q_ref[core] = q_own[...].T
    mem_copy.wait()
    p_copy.wait()
    q_copy.wait()
    new_ref[other] = mem_sib[...] - exact(p_sib[...], q_sib[...], NN)
    p_ref[other] = p_sib[...]
    q_ref[other] = q_sib[...].T


def compress(n_y, n_x, n_z, mem, seed):
    feat, width = mem.shape
    rank = seed.shape[1]
    slab = feat // 2
    n_rep = n_y * n_x
    dma = pltpu.SemaphoreType.DMA
    vmem = pl.BlockSpec(memory_space=pltpu.VMEM)
    f32 = jnp.float32
    return pl.pallas_call(
        functools.partial(compress_kernel, n_y, n_x, n_z),
        out_shape=(
            jax.ShapeDtypeStruct((2, slab, rank), f32),
            jax.ShapeDtypeStruct((2, width, rank), f32),
            jax.ShapeDtypeStruct((2, slab, width), f32),
        ),
        in_specs=[vmem] * 2,
        out_specs=[vmem] * 3,
        scratch_shapes=[
            pltpu.VMEM((slab, width), f32),
            pltpu.VMEM((n_x, slab, 2 * rank), f32),
            pltpu.VMEM((n_y, slab, 2 * rank), f32),
            pltpu.VMEM((n_z, rank // 2, 2 * rank), f32),
            pltpu.VMEM((n_rep, 8, width // 2), f32),
            pltpu.VMEM((n_rep, 8, width // 2), f32),
            pltpu.VMEM((n_z, 8, width // 2), f32),
            pltpu.VMEM((n_rep, 8, width // 2), f32),
            pltpu.VMEM((rank, 2 * rank), f32),
            pltpu.VMEM((rank, 2 * rank), f32),
            pltpu.VMEM((rank, width), f32),
            pltpu.VMEM((rank, width), f32),
            pltpu.VMEM((feat, rank), f32),
            pltpu.VMEM((slab, rank), f32),
            dma((n_x,)), dma((n_x,)),
            dma((n_y,)), dma((n_y,)),
            dma((n_z,)), dma((n_z,)),
            dma((n_rep,)), dma((n_rep,)),
            dma((n_z,)), dma((n_z,)),
            dma((n_rep,)), dma((n_rep,)),
            dma((3,)), dma((3,)),
        ],
        compiler_params=pltpu.CompilerParams(
            collective_id=1, has_side_effects=True, vmem_limit_bytes=32 * 1024 * 1024
        ),
        name="compress",
    )(mem, seed)


def shards(
    audio_hidden, score_hidden, audio_proj, score_proj, labels, q_seed, err_audio, err_score
):
    n_z = 8
    n_y = n_x = 4
    mem = head_gradient(
        n_z, audio_proj, score_proj, labels, audio_hidden, score_hidden, err_audio, err_score
    )
    p, q, new = compress(n_y, n_x, n_z, mem, q_seed)
    return (p[0], q[0], new[0:1], p[1], q[1], new[1:2])


def solution(mesh):
    placed = (
        P(("rep", "con"), None),
        P(("rep", "con"), None),
        P(("rep", "con"), None),
        P(("rep", "con"), None),
        P("rep", "con"),
        P(),
        P("rep", "con", None),
        P("rep", "con", None),
    )
    return jax.shard_map(
        shards,
        mesh=mesh,
        in_specs=placed,
        out_specs=(
            P("con", None),
            P(),
            P("rep", "con", None),
            P("con", None),
            P(),
            P("rep", "con", None),
        ),
        check_vma=False,
    )
```

```python
import functools

import jax
import jax.numpy as jnp
from jax import lax
from jax.experimental import pallas as pl
from jax.experimental.pallas import tpu as pltpu
from jax.sharding import PartitionSpec as P

MESH = pl.DeviceIdType.MESH
logit_scale = 30.0
NORM_EPS = 1e-06
LOG2E = 1.4426950408889634
NT = (((1,), (1,)), ((), ()))
TN = (((0,), (0,)), ((), ()))
NN = (((1,), (0,)), ((), ()))
HIGH = lax.Precision.HIGHEST

SLOT_OF = (0, 1, 3, 5, 7, 6, 4, 2)
BEHIND = (0, 1, 7, 2, 6, 3, 5, 4)
RING = (
    ((1, 0), (1, 1), (2, 0), (2, 1), (3, 0), (3, 1), (4, 0)),
    ((1, 1), (1, 0), (2, 1), (2, 0), (3, 1), (3, 0), (4, 1)),
)


def exact(left, right, dims):
    return lax.dot_general(
        left, right, dims, precision=HIGH, preferred_element_type=jnp.float32
    )


BOUNDS = ((0, 0), (960, 768), (1600, 1536), (2240, 2048), (2560, 2560))
ROW_TILE = (480, 400, 560, 640)


def whole_kernel(
    n_y, n_x, n_z, proj_a, proj_b, labels, hidden_a, hidden_b, err_a, err_b, seed,
    p_ref, q_ref, new_ref,
    raw, emb, logit, weight, grad, row_sum, col_sum, row_info, col_id, lab, pair, stage, blocks,
    hid, err, mem, mem_sib, x_buf, y_buf, g_buf, part, gathered, z_buf, full, full_sib,
    coeff, resid, basis, basis_sib, p_own, p_sib,
    ring_send, ring_recv, sib_send, sib_recv, lab_send, lab_recv, hid_send, hid_recv,
    near_send, near_recv, local_sem,
    x_send, x_recv, y_send, y_recv, g_send, g_recv, r_send, r_recv, z_send, z_recv,
    f_send, f_recv, pair_send, pair_recv,
):
    n_rep = n_y * n_x
    rank, width = seed.shape
    tok = proj_a.shape[0]
    chip = 2 * tok
    group = raw.shape[1]
    feat = hid.shape[1]
    slab = err_a.shape[1]
    rep = lax.axis_index("rep")
    con = lax.axis_index("con")
    y = rep // n_x
    x = lax.rem(rep, n_x)
    z = con // 2
    core = lax.rem(con, 2)
    other = 1 - core

    def plane(ahead):
        return (rep, lax.rem(z + ahead, n_z) * 2 + core)

    sibling = (rep, z * 2 + other)

    def along_x(i):
        return (y * n_x + lax.rem(x + i, n_x), con)

    def along_y(i):
        return (lax.rem(y + i, n_y) * n_x + x, con)

    def along_rep(i):
        return (lax.rem(rep + i, n_rep), con)

    projs = (proj_a, proj_b)
    loads = [
        pltpu.make_async_copy(projs[t], raw.at[t, pl.ds(0, tok), :], local_sem.at[t])
        for t in range(2)
    ]
    for load in loads:
        load.start()

    lab[0, 0] = jnp.zeros(lab.shape[2:], jnp.float32)
    lab[0, 0, :, 0:tok] = jnp.broadcast_to(labels[...].astype(jnp.float32), (8, tok))

    barrier = pltpu.get_barrier_semaphore()
    greet = [plane(1), plane(n_z - 1), sibling]
    greet += [along_x(i) for i in range(1, n_x)] + [along_y(i) for i in range(1, n_y)]
    for peer in greet:
        pl.semaphore_signal(barrier, inc=1, device_id=peer, device_id_type=MESH)
    pl.semaphore_wait(barrier, len(greet))
    for load in loads:
        load.wait()

    def remote(source, target, send, recv, peer):
        return pltpu.make_async_remote_copy(
            src_ref=source, dst_ref=target, send_sem=send, recv_sem=recv,
            device_id=peer, device_id_type=MESH,
        )

    def slot_at(way, dist):
        return SLOT_OF[dist] if way == 0 else SLOT_OF[(n_z - dist) % n_z]

    def ring(way, n):
        dist, t = RING[way][n]
        return remote(
            raw.at[t, pl.ds(slot_at(way, dist - 1) * chip, tok), :],
            raw.at[t, pl.ds(slot_at(way, dist) * chip, tok), :],
            ring_send.at[way, n],
            ring_recv.at[way, n],
            plane(1 if way == 0 else n_z - 1),
        )

    def sib(way, n):
        dist, t = RING[way][n] if n < 7 else (0, way)
        rows = slot_at(way, dist) * chip
        return remote(
            raw.at[t, pl.ds(rows, tok), :],
            raw.at[t, pl.ds(rows + tok, tok), :],
            sib_send.at[way, n],
            sib_recv.at[way, n],
            sibling,
        )

    def lab_copy(way, dist):
        return remote(
            lab.at[0, slot_at(way, dist - 1)], lab.at[0, slot_at(way, dist)],
            lab_send.at[way, dist - 1], lab_recv.at[way, dist - 1],
            plane(1 if way == 0 else n_z - 1),
        )

    def hid_copy(o):
        return remote(
            stage.at[lax.rem(z + o, n_z)], blocks.at[SLOT_OF[o]],
            hid_send.at[o], hid_recv.at[o], plane(o),
        )

    def lab_near():
        return remote(lab.at[0], lab.at[1], near_send.at[0], near_recv.at[0], sibling)

    def hid_near(source):
        return remote(source, pair.at[1], near_send.at[1], near_recv.at[1], sibling)

    def err_near(source):
        return remote(source.at[0], err.at[1], near_send.at[2], near_recv.at[2], sibling)

    def hid_local(source):
        return pltpu.make_async_copy(source, pair.at[0], local_sem.at[2])

    def err_local(source):
        return pltpu.make_async_copy(source.at[0], err.at[0], local_sem.at[3])

    def normalize(slot, cross, t):
        rows = pl.ds(slot * chip + cross * tok, tok)
        values = raw[t, rows, :].astype(jnp.float32)
        inverse = lax.rsqrt(jnp.sum(values * values, axis=1, keepdims=True) + NORM_EPS)
        emb[t, rows, :] = (values * inverse).astype(jnp.bfloat16)
        row_info[rows, t : t + 1] = inverse

    for way in range(2):
        lab_copy(way, 1).start()
    for n in range(2):
        for way in range(2):
            ring(way, n).start()
    for t in range(2):
        sib(t, 7).start()

    @pl.when(core == 0)
    def _():
        hid_near(hidden_b).start()
        hid_local(hidden_a).start()
        err_near(err_b).start()
        err_local(err_a).start()

    @pl.when(core == 1)
    def _():
        hid_near(hidden_a).start()
        hid_local(hidden_b).start()
        err_near(err_a).start()
        err_local(err_b).start()

    row_sum[...] = jnp.zeros_like(row_sum)
    col_sum[...] = jnp.zeros_like(col_sum)
    for t in range(2):
        normalize(0, 0, t)
    for t in range(2):
        sib(t, 7).wait_recv()
        normalize(0, 1, t)

    def tile_logits(r0, rows, c0, cols):
        left = emb[core, pl.ds(r0, rows), :]
        right = emb[other, pl.ds(c0, cols), :]
        part = jnp.exp2(
            (logit_scale * LOG2E)
            * lax.dot_general(left, right, NT, preferred_element_type=jnp.float32)
        )
        logit[pl.ds(r0, rows), pl.ds(c0, cols)] = part
        lanes = part[:, 0:128]
        for k in range(1, cols // 128):
            lanes = lanes + part[:, k * 128 : (k + 1) * 128]
        row_sum[pl.ds(r0, rows), :] += lanes
        col_sum[:, pl.ds(c0, cols)] += jnp.sum(part.reshape(rows // 8, 8, cols), axis=0)

    def logits_step(step):
        old_rows, old_cols = BOUNDS[step]
        new_rows, new_cols = BOUNDS[step + 1]
        cols = new_cols - old_cols
        rows = ROW_TILE[step]

        def columns(k, _):
            tile_logits(pl.multiple_of(k * rows, 16), rows, old_cols, cols)
            return 0

        lax.fori_loop(0, new_rows // rows, columns, 0)
        if old_cols:
            cut = 768 if step == 1 else 512

            def more(k, _):
                tile_logits(old_rows, new_rows - old_rows, pl.multiple_of(k * cut, 256), cut)
                return 0

            lax.fori_loop(0, old_cols // cut, more, 0)

    wide = stage.shape[2]
    narrow = feat - wide
    part_rows = chip * narrow // wide

    def pack():
        for half in range(2):
            for k in range(n_z):
                first = k * feat
                stage[k, half * tok : (half + 1) * tok, :] = pair[half, :, first : first + wide]
                for g in range(tok // part_rows):
                    lane = (half * (tok // part_rows) + g) * narrow
                    stage[k, chip : chip + part_rows, lane : lane + narrow] = pair[
                        half, g * part_rows : (g + 1) * part_rows, first + wide : first + feat
                    ]

    def unpack(slot, block):
        rows = slot * chip
        hid[rows : rows + chip, 0:wide] = block[0:chip, :]
        for g in range(chip // part_rows):
            hid[rows + g * part_rows : rows + (g + 1) * part_rows, wide:feat] = block[
                chip : chip + part_rows, g * narrow : (g + 1) * narrow
            ]

    def pair_ids():
        for slot in range(n_z):
            where = lax.rem(z + n_z - BEHIND[slot], n_z)
            for r in range(2):
                first = ((where * 2 + (other if r else core)) * tok).astype(jnp.float32)
                piece = lab[r, slot]
                spread = jnp.broadcast_to(piece[0:1, :], (128, piece.shape[1])).T[:tok, 0:1]
                own = first + lax.broadcasted_iota(jnp.int32, (tok, 1), 0).astype(jnp.float32)
                rows = pl.ds(slot * chip + r * tok, tok)
                row_info[rows, 2:3] = jnp.where(core == 0, spread, own)
                row_info[rows, 3:4] = jnp.where(core == 0, own, spread)
        for k in range(group // 128):
            ids = row_info[k * 128 : (k + 1) * 128, 3:4]
            col_id[:, k * 128 : (k + 1) * 128] = jnp.broadcast_to(ids, (128, 128)).T[0:8, :]

    last = len(RING[0])
    for n in range(last):
        for way in range(2):
            ring(way, n).wait_recv()
            if n < (4, 3)[way]:
                lab_copy(way, n + 1).wait_recv()
            if n + 2 <= (4, 3)[way]:
                lab_copy(way, n + 2).start()
            if n + 2 < last:
                ring(way, n + 2).start()
            sib(way, n).start()
        if n == last - 1:
            for o in range(1, n_z):
                hid_copy(o).start()
        for way in range(2):
            dist, t = RING[way][n]
            normalize(slot_at(way, dist), 0, t)
        if n == 0:
            hid_near(hidden_a).wait_recv()
            hid_local(hidden_a).wait()
            pack()
        if n == 3:
            lab_near().start()
        for way in range(2):
            dist, t = RING[way][n]
            sib(way, n).wait_recv()
            normalize(slot_at(way, dist), 1, t)
        if n % 2:
            logits_step(n // 2)
        if n == 4:
            lab_near().wait_recv()
            pair_ids()
    logits_step(3)

    row_info[:, 4:5] = 0.5 / jnp.sum(row_sum[...], axis=1, keepdims=True)
    col_sum[0:1, :] = 0.5 / jnp.sum(col_sum[...], axis=0, keepdims=True)
    row_info[:, 5:6] = jnp.where(core == 0, row_info[:, 0:1], row_info[:, 1:2])

    chunk = weight.shape[0]
    fine = 16

    def chunk_step(k, _):
        r0 = pl.multiple_of(k * chunk, chunk)
        for m in range(chunk // fine):
            rows = pl.ds(r0 + m * fine, fine)
            value = logit[rows, :] * (row_info[rows, 4:5] + col_sum[0:1, :])
            value = value - jnp.where(row_info[rows, 2:3] == col_id[0:1, :], 1.0, 0.0)
            weight[m * fine : (m + 1) * fine, :] = value.astype(jnp.bfloat16)
        grad[...] = lax.dot_general(
            weight[...], emb[other], NN, preferred_element_type=jnp.float32
        )
        for m in range(chunk // fine):
            rows = pl.ds(r0 + m * fine, fine)
            inverse = row_info[rows, 5:6]
            unit = raw[core, rows, :].astype(jnp.float32) * inverse
            value = logit_scale * grad[m * fine : (m + 1) * fine, :]
            along = jnp.sum(unit * value, axis=1, keepdims=True)
            emb[core, rows, :] = ((value - unit * along) * inverse).astype(jnp.bfloat16)
        return 0

    lax.fori_loop(0, group // chunk, chunk_step, 0)

    unpack(0, stage.at[z])
    for o in range(1, n_z):
        hid_copy(o).wait_recv()
        unpack(SLOT_OF[o], blocks.at[SLOT_OF[o]])
    err_near(err_a).wait_recv()
    err_local(err_a).wait()
    total = lax.dot_general(hid[...], emb[core], TN, preferred_element_type=jnp.float32)
    for k in range(2):
        rows = slice(k * slab, (k + 1) * slab)
        mem[rows, :] = total[rows, :] + err[jnp.where(core == k, 0, 1)]

    theirs = pl.ds(pl.multiple_of(other * slab, 8), slab)
    ours = pl.ds(pl.multiple_of(core * slab, 8), slab)
    mem_copy = remote(mem.at[theirs, :], mem_sib, pair_send.at[0], pair_recv.at[0], sibling)
    mem_copy.start()

    def all_sum(buf, index, count, send, recv, peers, value):
        buf[index] = value
        copies = [
            remote(buf.at[index], buf.at[index], send.at[i], recv.at[i], peers(i))
            for i in range(1, count)
        ]
        for one in copies:
            one.start()

        def finish():
            for one in copies:
                one.wait()
            total = buf[0]
            for k in range(1, count):
                total = total + buf[k]
            return total

        return finish

    left = exact(seed[...], mem[...], NT)
    strip = rank // 4
    packed = jnp.concatenate(
        [left[:, :128]]
        + [jnp.concatenate([left[g * strip : (g + 1) * strip, 128:] for g in range(4)], axis=1)],
        axis=0,
    )
    packed = all_sum(x_buf, x, n_x, x_send, x_recv, along_x, packed)()
    packed = all_sum(y_buf, y, n_y, y_send, y_recv, along_y, packed)()
    tail = [packed[rank:, g * 32 : (g + 1) * 32] for g in range(4)]
    left = jnp.concatenate([packed[:rank, :], jnp.concatenate(tail, axis=0)], axis=1)

    gram = exact(left, left, NT)
    gram_sum = all_sum(
        g_buf, z, n_z, g_send, g_recv, plane,
        jnp.concatenate([gram[: rank // 2, :], gram[rank // 2 :, :]], axis=1),
    )
    right = exact(left, mem[...], NN)
    span = width // 2
    for k in range(n_rep):
        part[k] = right[8 * (k // 2) : 8 * (k // 2) + 8, span * (k % 2) : span * (k % 2) + span]
    gathered[rep] = part[rep]
    reduce = [
        remote(
            part.at[lax.rem(rep + i, n_rep)], gathered.at[rep], r_send.at[i], r_recv.at[i],
            along_rep(i),
        )
        for i in range(1, n_rep)
    ]
    for one in reduce:
        one.start()

    gram = gram_sum()
    resid[...] = jnp.concatenate([gram[:, :rank], gram[:, rank:]], axis=0)
    coeff[...] = (
        lax.broadcasted_iota(jnp.int32, (rank, rank), 0)
        == lax.broadcasted_iota(jnp.int32, (rank, rank), 1)
    ).astype(jnp.float32)

    def column_step(k, _):
        lane = lax.broadcasted_iota(jnp.int32, (rank, rank), 1)
        u = coeff[pl.ds(k, 1), :]
        w = resid[pl.ds(k, 1), :]
        values = resid[...]
        square = jnp.maximum(jnp.sum(u * w, axis=1, keepdims=True), 0.0) + NORM_EPS
        column = jnp.sum(jnp.where(lane == k, values, 0.0), axis=1, keepdims=True)
        inverse = 1.0 / square
        basis[pl.ds(k, 1), :] = u * lax.rsqrt(square)
        coeff[...] -= column * (u * inverse)
        resid[...] = values - column * (w * inverse)
        return 0

    cuts = [0, rank // 3, 2 * rank // 3, rank]
    lax.fori_loop(cuts[0], cuts[1], column_step, 0)
    for one in reduce:
        one.wait()
    total = gathered[0]
    for k in range(1, n_rep):
        total = total + gathered[k]
    z_sum = all_sum(z_buf, z, n_z, z_send, z_recv, plane, total)
    lax.fori_loop(cuts[1], cuts[2], column_step, 0)
    full[rep] = z_sum()
    spread = [
        remote(full.at[rep], full.at[rep], f_send.at[i], f_recv.at[i], along_rep(i))
        for i in range(1, n_rep)
    ]
    for one in spread:
        one.start()
    lax.fori_loop(cuts[2], cuts[3], column_step, 0)

    turn_copy = remote(basis, basis_sib, pair_send.at[2], pair_recv.at[2], sibling)
    turn_copy.start()
    turn = basis[...]
    factor = exact(turn, left, NN)
    for k in range(2):
        p_own[k] = factor[:, k * slab : (k + 1) * slab]
    p_copy = remote(p_own.at[other], p_sib, pair_send.at[1], pair_recv.at[1], sibling)
    p_copy.start()
    for one in spread:
        one.wait_recv()
    full_copy = remote(full, full_sib, pair_send.at[3], pair_recv.at[3], sibling)
    full_copy.start()

    def finish(head, turn, blocks, memory, factor):
        right = jnp.concatenate(
            [
                jnp.concatenate([blocks[2 * k], blocks[2 * k + 1]], axis=1)
                for k in range(n_rep // 2)
            ],
            axis=0,
        )
        right = exact(turn, right, NN) / n_rep
        q_ref[head] = right
        p_ref[head] = factor
        new_ref[head] = memory - exact(factor, right, TN)

    finish(core, turn, full, mem[ours, :], p_own[core])
    mem_copy.wait()
    p_copy.wait()
    turn_copy.wait()
    full_copy.wait()
    finish(other, basis_sib[...], full_sib, mem_sib[...], p_sib[...])
    for one in spread:
        one.wait_send()

    for way in range(2):
        for n in range(last):
            ring(way, n).wait_send()
        for n in range(last + 1):
            sib(way, n).wait_send()
        for dist in range(1, (5, 4)[way]):
            lab_copy(way, dist).wait_send()
    for o in range(1, n_z):
        hid_copy(o).wait_send()
    lab_near().wait_send()
    hid_near(hidden_a).wait_send()
    err_near(err_a).wait_send()


def whole(n_y, n_x, n_z, proj_a, proj_b, labels, hidden_a, hidden_b, err_a, err_b, seed):
    tok, width = proj_a.shape
    rank = seed.shape[0]
    group = tok * n_z * 2
    feat = hidden_a.shape[1] // n_z
    slab = err_a.shape[1]
    n_rep = n_y * n_x
    chunk = 256
    packed = 2 * tok * feat // 128
    dma = pltpu.SemaphoreType.DMA
    any_space = pl.BlockSpec(memory_space=pl.ANY)
    vmem = pl.BlockSpec(memory_space=pltpu.VMEM)
    f32 = jnp.float32
    return pl.pallas_call(
        functools.partial(whole_kernel, n_y, n_x, n_z),
        out_shape=(
            jax.ShapeDtypeStruct((2, rank, slab), f32),
            jax.ShapeDtypeStruct((2, rank, width), f32),
            jax.ShapeDtypeStruct((2, slab, width), f32),
        ),
        in_specs=[any_space, any_space, vmem] + [any_space] * 4 + [vmem],
        out_specs=[vmem] * 3,
        scratch_shapes=[
            pltpu.VMEM((2, group, width), jnp.bfloat16),
            pltpu.VMEM((2, group, width), jnp.bfloat16),
            pltpu.VMEM((group, group), f32),
            pltpu.VMEM((chunk, group), jnp.bfloat16),
            pltpu.VMEM((chunk, width), f32),
            pltpu.VMEM((group, 128), f32),
            pltpu.VMEM((8, group), f32),
            pltpu.VMEM((group, 128), f32),
            pltpu.VMEM((8, group), f32),
            pltpu.VMEM((2, n_z, 8, 256), f32),
            pltpu.VMEM((2, tok, feat * n_z), jnp.bfloat16),
            pltpu.VMEM((n_z, packed, 128), jnp.bfloat16),
            pltpu.VMEM((n_z, packed, 128), jnp.bfloat16),
            pltpu.VMEM((group, feat), jnp.bfloat16),
            pltpu.VMEM((2, slab, width), f32),
            pltpu.VMEM((feat, width), f32),
            pltpu.VMEM((slab, width), f32),
            pltpu.VMEM((n_x, slab, 2 * rank), f32),
            pltpu.VMEM((n_y, slab, 2 * rank), f32),
            pltpu.VMEM((n_z, rank // 2, 2 * rank), f32),
            pltpu.VMEM((n_rep, 8, width // 2), f32),
            pltpu.VMEM((n_rep, 8, width // 2), f32),
            pltpu.VMEM((n_z, 8, width // 2), f32),
            pltpu.VMEM((n_rep, 8, width // 2), f32),
            pltpu.VMEM((n_rep, 8, width // 2), f32),
            pltpu.VMEM((rank, rank), f32),
            pltpu.VMEM((rank, rank), f32),
            pltpu.VMEM((rank, rank), f32),
            pltpu.VMEM((rank, rank), f32),
            pltpu.VMEM((2, rank, slab), f32),
            pltpu.VMEM((rank, slab), f32),
            dma((2, 7)), dma((2, 7)),
            dma((2, 8)), dma((2, 8)),
            dma((2, 4)), dma((2, 4)),
            dma((n_z,)), dma((n_z,)),
            dma((3,)), dma((3,)),
            dma((4,)),
            dma((n_x,)), dma((n_x,)),
            dma((n_y,)), dma((n_y,)),
            dma((n_z,)), dma((n_z,)),
            dma((n_rep,)), dma((n_rep,)),
            dma((n_z,)), dma((n_z,)),
            dma((n_rep,)), dma((n_rep,)),
            dma((4,)), dma((4,)),
        ],
        compiler_params=pltpu.CompilerParams(
            collective_id=0, has_side_effects=True, vmem_limit_bytes=63 * 1024 * 1024
        ),
        name="whole",
    )(proj_a, proj_b, labels, hidden_a, hidden_b, err_a, err_b, seed)


def shards(
    audio_hidden, score_hidden, audio_proj, score_proj, labels, q_seed, err_audio, err_score
):
    n_z = 8
    n_y = n_x = 4
    p, q, new = whole(
        n_y, n_x, n_z, audio_proj, score_proj, labels, audio_hidden, score_hidden,
        err_audio, err_score, q_seed.T,
    )
    return (p[0].T, q[0].T, new[0:1], p[1].T, q[1].T, new[1:2])


def solution(mesh):
    placed = (
        P(("rep", "con"), None),
        P(("rep", "con"), None),
        P(("rep", "con"), None),
        P(("rep", "con"), None),
        P("rep", "con"),
        P(),
        P("rep", "con", None),
        P("rep", "con", None),
    )
    return jax.shard_map(
        shards,
        mesh=mesh,
        in_specs=placed,
        out_specs=(
            P("con", None),
            P(),
            P("rep", "con", None),
            P("con", None),
            P(),
            P("rep", "con", None),
        ),
        check_vma=False,
    )
```

```python
import functools

import jax
import jax.numpy as jnp
from jax import lax
from jax.experimental import pallas as pl
from jax.experimental.pallas import tpu as pltpu
from jax.sharding import PartitionSpec as P

MESH = pl.DeviceIdType.MESH
logit_scale = 30.0
NORM_EPS = 1e-06
LOG2E = 1.4426950408889634
NT = (((1,), (1,)), ((), ()))
TN = (((0,), (0,)), ((), ()))
NN = (((1,), (0,)), ((), ()))
HIGH = lax.Precision.HIGHEST

SLOT_OF = (0, 1, 3, 5, 7, 6, 4, 2)
BEHIND = (0, 1, 7, 2, 6, 3, 5, 4)
RING = (
    ((1, 0), (1, 1), (2, 0), (2, 1), (3, 0), (3, 1), (4, 0), (4, 0)),
    ((1, 1), (1, 0), (2, 1), (2, 0), (3, 1), (3, 0), (4, 1), (4, 1)),
)
FAR = 7


def exact(left, right, dims):
    return lax.dot_general(
        left, right, dims, precision=HIGH, preferred_element_type=jnp.float32
    )


OWN = 8

BOUNDS = ((0, 0), (960, 768), (1600, 1536), (2240, 2048), (2400, 2304), (2560, 2560))
ROW_TILE = (480, 400, 560, 600, 640)
COL_TILE = (0, 768, 512, 512, 768)


def whole_kernel(
    n_y, n_x, n_z, proj_a, proj_b, labels, hidden_a, hidden_b, err_a, err_b, seed,
    p_ref, q_ref, mem_ref,
    raw, emb, logit, weight, grad, col_sum, row_info, col_id, lab, pair, stage, blocks,
    hid, err, mem, mem_sib, x_buf, y_buf, g_buf, part, gathered, z_buf, full, full_sib,
    coeff, resid, basis, basis_sib, p_own, p_sib,
    ring_send, ring_recv, sib_send, sib_recv, lab_send, lab_recv, hid_send, hid_recv,
    near_send, near_recv, local_sem,
    x_send, x_recv, y_send, y_recv, g_send, g_recv, r_send, r_recv, z_send, z_recv,
    f_send, f_recv, pair_send, pair_recv,
):
    n_rep = n_y * n_x
    rank, width = seed.shape
    tok = proj_a.shape[0]
    chip = 2 * tok
    group = raw.shape[1]
    feat = hid.shape[1]
    slab = err_a.shape[1]
    rep = lax.axis_index("rep")
    con = lax.axis_index("con")
    y = rep // n_x
    x = lax.rem(rep, n_x)
    z = con // 2
    core = lax.rem(con, 2)
    other = 1 - core

    def plane(ahead):
        return (rep, lax.rem(z + ahead, n_z) * 2 + core)

    sibling = (rep, z * 2 + other)

    def along_x(i):
        return (y * n_x + lax.rem(x + i, n_x), con)

    def along_y(i):
        return (lax.rem(y + i, n_y) * n_x + x, con)

    def along_rep(i):
        return (lax.rem(rep + i, n_rep), con)

    projs = (proj_a, proj_b)
    loads = [
        pltpu.make_async_copy(projs[t], raw.at[t, pl.ds(0, tok), :], local_sem.at[t])
        for t in range(2)
    ]
    for load in loads:
        load.start()

    lab[0, 0] = jnp.zeros(lab.shape[2:], jnp.float32)
    lab[0, 0, :, 0:tok] = jnp.broadcast_to(labels[...].astype(jnp.float32), (8, tok))

    barrier = pltpu.get_barrier_semaphore()
    greet = [plane(1), plane(n_z - 1), sibling]
    greet += [along_x(i) for i in range(1, n_x)] + [along_y(i) for i in range(1, n_y)]
    for peer in greet:
        pl.semaphore_signal(barrier, inc=1, device_id=peer, device_id_type=MESH)
    pl.semaphore_wait(barrier, len(greet))
    for load in loads:
        load.wait()

    def remote(source, target, send, recv, peer):
        return pltpu.make_async_remote_copy(
            src_ref=source, dst_ref=target, send_sem=send, recv_sem=recv,
            device_id=peer, device_id_type=MESH,
        )

    def slot_at(way, dist):
        return SLOT_OF[dist] if way == 0 else SLOT_OF[(n_z - dist) % n_z]

    half = tok // 2

    def place(slot, cross, part):
        if slot == FAR:
            return slot * chip + (part * 2 + cross) * half, half
        return slot * chip + cross * tok, tok

    def item(way, n):
        dist, t = RING[way][n]
        return dist, t, slot_at(way, dist), (n - 6 if dist == 4 else 0)

    def ring(way, n):
        dist, t, slot, part = item(way, n)
        first, rows = place(slot, 0, part)
        source = place(slot_at(way, dist - 1), 0, 0)[0] + part * half
        return remote(
            raw.at[t, pl.ds(source, rows), :],
            raw.at[t, pl.ds(first, rows), :],
            ring_send.at[way, n],
            ring_recv.at[way, n],
            plane(1 if way == 0 else n_z - 1),
        )

    def sib(way, n):
        dist, t, slot, part = item(way, n) if n < OWN else (0, way, 0, 0)
        first, rows = place(slot, 0, part)
        target, _ = place(slot, 1, part)
        return remote(
            raw.at[t, pl.ds(first, rows), :],
            raw.at[t, pl.ds(target, rows), :],
            sib_send.at[way, n],
            sib_recv.at[way, n],
            sibling,
        )

    def lab_copy(way, dist):
        return remote(
            lab.at[0, slot_at(way, dist - 1)], lab.at[0, slot_at(way, dist)],
            lab_send.at[way, dist - 1], lab_recv.at[way, dist - 1],
            plane(1 if way == 0 else n_z - 1),
        )

    def hid_copy(o):
        return remote(
            stage.at[lax.rem(z + o, n_z)], blocks.at[SLOT_OF[o]],
            hid_send.at[o], hid_recv.at[o], plane(o),
        )

    def lab_near():
        return remote(lab.at[0], lab.at[1], near_send.at[0], near_recv.at[0], sibling)

    def hid_near(source):
        return remote(source, pair.at[1], near_send.at[1], near_recv.at[1], sibling)

    def err_near(source):
        return remote(source.at[0], err.at[1], near_send.at[2], near_recv.at[2], sibling)

    def hid_local(source):
        return pltpu.make_async_copy(source, pair.at[0], local_sem.at[2])

    def err_local(source):
        return pltpu.make_async_copy(source.at[0], err.at[0], local_sem.at[3])

    def normalize(slot, cross, t, part=0):
        first, count = place(slot, cross, part)
        rows = pl.ds(first, count)
        values = raw[t, rows, :].astype(jnp.float32)
        inverse = lax.rsqrt(jnp.sum(values * values, axis=1, keepdims=True) + NORM_EPS)
        emb[t, rows, :] = (values * inverse).astype(jnp.bfloat16)
        row_info[rows, t : t + 1] = inverse

    for way in range(2):
        lab_copy(way, 1).start()
    for n in range(2):
        for way in range(2):
            ring(way, n).start()
    for t in range(2):
        sib(t, OWN).start()

    @pl.when(core == 0)
    def _():
        hid_near(hidden_b).start()
        hid_local(hidden_a).start()
        err_near(err_b).start()
        err_local(err_a).start()

    @pl.when(core == 1)
    def _():
        hid_near(hidden_a).start()
        hid_local(hidden_b).start()
        err_near(err_a).start()
        err_local(err_b).start()

    row_info[...] = jnp.zeros_like(row_info)
    col_sum[...] = jnp.zeros_like(col_sum)
    for t in range(2):
        normalize(0, 0, t)
    for t in range(2):
        sib(t, OWN).wait_recv()
        normalize(0, 1, t)

    def tile_logits(r0, rows, c0, cols):
        left = emb[core, pl.ds(r0, rows), :]
        right = emb[other, pl.ds(c0, cols), :]
        part = jnp.exp2(
            (logit_scale * LOG2E)
            * lax.dot_general(left, right, NT, preferred_element_type=jnp.float32)
        )
        logit[pl.ds(r0, rows), pl.ds(c0, cols)] = part
        lanes = part[:, 0:128]
        for k in range(1, cols // 128):
            lanes = lanes + part[:, k * 128 : (k + 1) * 128]
        row_info[pl.ds(r0, rows), 6:7] += jnp.sum(lanes, axis=1, keepdims=True)
        col_sum[:, pl.ds(c0, cols)] += jnp.sum(part.reshape(rows // 8, 8, cols), axis=0)

    def logits_step(step):
        old_rows, old_cols = BOUNDS[step]
        new_rows, new_cols = BOUNDS[step + 1]
        cols = new_cols - old_cols
        rows = ROW_TILE[step]

        def columns(k, _):
            tile_logits(pl.multiple_of(k * rows, 16), rows, old_cols, cols)
            return 0

        def more(k, _):
            first = pl.multiple_of(k * COL_TILE[step], 256)
            tile_logits(old_rows, new_rows - old_rows, first, COL_TILE[step])
            return 0

        if step < 2:
            lax.fori_loop(0, new_rows // rows, columns, 0)
        else:
            for k in range(new_rows // rows):
                tile_logits(k * rows, rows, old_cols, cols)
        if step == 2:
            late_rows(other)
        elif step == 1:
            lax.fori_loop(0, old_cols // COL_TILE[step], more, 0)
        elif old_cols:
            for k in range(old_cols // COL_TILE[step]):
                tile_logits(old_rows, new_rows - old_rows, k * COL_TILE[step], COL_TILE[step])

    def late_rows(which):
        first = pl.multiple_of(5 * chip + which * chip, 16)
        for k in range(BOUNDS[2][1] // COL_TILE[2]):
            tile_logits(first, chip, k * COL_TILE[2], COL_TILE[2])

    wide = stage.shape[2]
    narrow = feat - wide
    part_rows = chip * narrow // wide

    def pack():
        for half in range(2):
            for k in range(n_z):
                first = k * feat
                stage[k, half * tok : (half + 1) * tok, :] = pair[half, :, first : first + wide]
                for g in range(tok // part_rows):
                    lane = (half * (tok // part_rows) + g) * narrow
                    stage[k, chip : chip + part_rows, lane : lane + narrow] = pair[
                        half, g * part_rows : (g + 1) * part_rows, first + wide : first + feat
                    ]

    def unpack(slot, block):
        for g in range(chip // part_rows):
            cross, part = g // 2, g % 2
            first = place(slot, cross, part)[0] + (0 if slot == FAR else part * half)
            source = slice(g * part_rows, (g + 1) * part_rows)
            hid[first : first + part_rows, 0:wide] = block[source, :]
            hid[first : first + part_rows, wide:feat] = block[
                chip : chip + part_rows, g * narrow : (g + 1) * narrow
            ]

    def pair_ids():
        for slot in range(n_z):
            where = lax.rem(z + n_z - BEHIND[slot], n_z)
            for r in range(2):
                first = ((where * 2 + (other if r else core)) * tok).astype(jnp.float32)
                piece = lab[r, slot]
                spread = jnp.broadcast_to(piece[0:1, :], (128, piece.shape[1])).T[:tok, 0:1]
                own = first + lax.broadcasted_iota(jnp.int32, (tok, 1), 0).astype(jnp.float32)
                ids_row = jnp.where(core == 0, spread, own)
                ids_col = jnp.where(core == 0, own, spread)
                for part in range(2):
                    start = place(slot, r, part)[0] + (0 if slot == FAR else part * half)
                    source = slice(part * half, (part + 1) * half)
                    row_info[start : start + half, 2:3] = ids_row[source, :]
                    row_info[start : start + half, 3:4] = ids_col[source, :]
        for k in range(group // 128):
            ids = row_info[k * 128 : (k + 1) * 128, 3:4]
            col_id[:, k * 128 : (k + 1) * 128] = jnp.broadcast_to(ids, (128, 128)).T[0:8, :]

    last = len(RING[0])
    for n in range(last):
        for way in range(2):
            ring(way, n).wait_recv()
            if n < (4, 3)[way]:
                lab_copy(way, n + 1).wait_recv()
            if n + 2 <= (4, 3)[way]:
                lab_copy(way, n + 2).start()
            if n < 5:
                ring(way, n + 2).start()
            if n == 5:
                ring(way, 7).start()
            sib(way, n).start()
        if n == 6:
            for o in range(1, n_z):
                hid_copy(o).start()
        for way in range(2):
            _, t, slot, end = item(way, n)
            normalize(slot, 0, t, end)
        if n == 0:
            hid_near(hidden_a).wait_recv()
            hid_local(hidden_a).wait()
            pack()
        if n == 3:
            lab_near().start()
        for way in range(2):
            _, t, slot, end = item(way, n)
            sib(way, n).wait_recv()
            normalize(slot, 1, t, end)
        if n in (1, 3, 5):
            logits_step(n // 2)
        if n == 4:
            lab_near().wait_recv()
            pair_ids()
            late_rows(core)
        if n >= 6:
            logits_step(n - 3)

    row_info[:, 4:5] = 0.5 / row_info[:, 6:7]
    col_sum[0:1, :] = 0.5 / jnp.sum(col_sum[...], axis=0, keepdims=True)
    row_info[:, 5:6] = jnp.where(core == 0, row_info[:, 0:1], row_info[:, 1:2])

    chunk = weight.shape[0]
    fine = 16

    def chunk_step(k, _):
        r0 = pl.multiple_of(k * chunk, chunk)
        for m in range(chunk // fine):
            rows = pl.ds(r0 + m * fine, fine)
            value = logit[rows, :] * (row_info[rows, 4:5] + col_sum[0:1, :])
            value = value - jnp.where(row_info[rows, 2:3] == col_id[0:1, :], 1.0, 0.0)
            weight[m * fine : (m + 1) * fine, :] = value.astype(jnp.bfloat16)
        grad[...] = lax.dot_general(
            weight[...], emb[other], NN, preferred_element_type=jnp.float32
        )
        for m in range(chunk // fine):
            rows = pl.ds(r0 + m * fine, fine)
            inverse = row_info[rows, 5:6]
            unit = raw[core, rows, :].astype(jnp.float32) * inverse
            value = logit_scale * grad[m * fine : (m + 1) * fine, :]
            along = jnp.sum(unit * value, axis=1, keepdims=True)
            emb[core, rows, :] = ((value - unit * along) * inverse).astype(jnp.bfloat16)
        return 0

    lax.fori_loop(0, group // chunk, chunk_step, 0)
    for o in range(1, n_z):
        hid_copy(o).wait_recv()
    err_near(err_a).wait_recv()
    err_local(err_a).wait()
    unpack(0, stage.at[z])
    for o in range(1, n_z):
        unpack(SLOT_OF[o], blocks.at[SLOT_OF[o]])
    total = lax.dot_general(hid[...], emb[core], TN, preferred_element_type=jnp.float32)
    for k in range(2):
        rows = slice(k * slab, (k + 1) * slab)
        mem[rows, :] = total[rows, :] + err[jnp.where(core == k, 0, 1)]

    theirs = pl.ds(pl.multiple_of(other * slab, 8), slab)
    ours = pl.ds(pl.multiple_of(core * slab, 8), slab)
    mem_copy = remote(mem.at[theirs, :], mem_sib, pair_send.at[0], pair_recv.at[0], sibling)
    mem_copy.start()

    def all_sum(buf, index, count, send, recv, peers, value):
        buf[index] = value
        copies = [
            remote(buf.at[index], buf.at[index], send.at[i], recv.at[i], peers(i))
            for i in range(1, count)
        ]
        for one in copies:
            one.start()

        def finish():
            for one in copies:
                one.wait()
            total = buf[0]
            for k in range(1, count):
                total = total + buf[k]
            return total

        return finish

    left = exact(seed[...], mem[...], NT)
    strip = rank // 4
    packed = jnp.concatenate(
        [left[:, :128]]
        + [jnp.concatenate([left[g * strip : (g + 1) * strip, 128:] for g in range(4)], axis=1)],
        axis=0,
    )
    packed = all_sum(x_buf, x, n_x, x_send, x_recv, along_x, packed)()
    packed = all_sum(y_buf, y, n_y, y_send, y_recv, along_y, packed)()
    tail = [packed[rank:, g * 32 : (g + 1) * 32] for g in range(4)]
    left = jnp.concatenate([packed[:rank, :], jnp.concatenate(tail, axis=0)], axis=1)

    gram = exact(left, left, NT)
    gram_sum = all_sum(
        g_buf, z, n_z, g_send, g_recv, plane,
        jnp.concatenate([gram[: rank // 2, :], gram[rank // 2 :, :]], axis=1),
    )
    right = exact(left, mem[...], NN)
    span = width // 2
    for k in range(n_rep):
        part[k] = right[8 * (k // 2) : 8 * (k // 2) + 8, span * (k % 2) : span * (k % 2) + span]
    gathered[rep] = part[rep]
    reduce = [
        remote(
            part.at[lax.rem(rep + i, n_rep)], gathered.at[rep], r_send.at[i], r_recv.at[i],
            along_rep(i),
        )
        for i in range(1, n_rep)
    ]
    for one in reduce:
        one.start()

    gram = gram_sum()
    resid[...] = jnp.concatenate([gram[:, :rank], gram[:, rank:]], axis=0)
    coeff[...] = (
        lax.broadcasted_iota(jnp.int32, (rank, rank), 0)
        == lax.broadcasted_iota(jnp.int32, (rank, rank), 1)
    ).astype(jnp.float32)

    def column_step(k, _):
        lane = lax.broadcasted_iota(jnp.int32, (rank, rank), 1)
        u = coeff[pl.ds(k, 1), :]
        w = resid[pl.ds(k, 1), :]
        values = resid[...]
        square = jnp.maximum(jnp.sum(u * w, axis=1, keepdims=True), 0.0) + NORM_EPS
        column = jnp.sum(jnp.where(lane == k, values, 0.0), axis=1, keepdims=True)
        inverse = 1.0 / square
        basis[pl.ds(k, 1), :] = u * lax.rsqrt(square)
        coeff[...] -= column * (u * inverse)
        resid[...] = values - column * (w * inverse)
        return 0

    cuts = [0, rank // 3, 2 * rank // 3, rank]
    lax.fori_loop(cuts[0], cuts[1], column_step, 0)
    for one in reduce:
        one.wait()
    total = gathered[0]
    for k in range(1, n_rep):
        total = total + gathered[k]
    z_sum = all_sum(z_buf, z, n_z, z_send, z_recv, plane, total)
    lax.fori_loop(cuts[1], cuts[2], column_step, 0)
    full[rep] = z_sum()
    spread = [
        remote(full.at[rep], full.at[rep], f_send.at[i], f_recv.at[i], along_rep(i))
        for i in range(1, n_rep)
    ]
    for one in spread:
        one.start()
    lax.fori_loop(cuts[2], cuts[3], column_step, 0)

    turn_copy = remote(basis, basis_sib, pair_send.at[2], pair_recv.at[2], sibling)
    turn_copy.start()
    turn = basis[...]
    factor = exact(turn, left, NN)
    for k in range(2):
        p_own[k] = factor[:, k * slab : (k + 1) * slab]
    p_copy = remote(p_own.at[other], p_sib, pair_send.at[1], pair_recv.at[1], sibling)
    p_copy.start()
    for one in spread:
        one.wait_recv()
    full_copy = remote(full, full_sib, pair_send.at[3], pair_recv.at[3], sibling)
    full_copy.start()

    def finish(head, turn, blocks, memory, factor):
        right = jnp.concatenate(
            [
                jnp.concatenate([blocks[2 * k], blocks[2 * k + 1]], axis=1)
                for k in range(n_rep // 2)
            ],
            axis=0,
        )
        right = exact(turn, right, NN) / n_rep
        q_ref[head] = right
        p_ref[head] = factor
        mem_ref[head] = memory

    finish(core, turn, full, mem[ours, :], p_own[core])
    mem_copy.wait()
    p_copy.wait()
    turn_copy.wait()
    full_copy.wait()
    finish(other, basis_sib[...], full_sib, mem_sib[...], p_sib[...])
    for one in spread:
        one.wait_send()

    for way in range(2):
        for n in range(last):
            ring(way, n).wait_send()
        for n in range(last + 1):
            sib(way, n).wait_send()
        for dist in range(1, (5, 4)[way]):
            lab_copy(way, dist).wait_send()
    for o in range(1, n_z):
        hid_copy(o).wait_send()
    lab_near().wait_send()
    hid_near(hidden_a).wait_send()
    err_near(err_a).wait_send()


def whole(n_y, n_x, n_z, proj_a, proj_b, labels, hidden_a, hidden_b, err_a, err_b, seed):
    tok, width = proj_a.shape
    rank = seed.shape[0]
    group = tok * n_z * 2
    feat = hidden_a.shape[1] // n_z
    slab = err_a.shape[1]
    n_rep = n_y * n_x
    chunk = 256
    packed = 2 * tok * feat // 128
    dma = pltpu.SemaphoreType.DMA
    any_space = pl.BlockSpec(memory_space=pl.ANY)
    vmem = pl.BlockSpec(memory_space=pltpu.VMEM)
    f32 = jnp.float32
    return pl.pallas_call(
        functools.partial(whole_kernel, n_y, n_x, n_z),
        out_shape=(
            jax.ShapeDtypeStruct((2, rank, slab), f32),
            jax.ShapeDtypeStruct((2, rank, width), f32),
            jax.ShapeDtypeStruct((2, slab, width), f32),
        ),
        in_specs=[any_space, any_space, vmem] + [any_space] * 4 + [vmem],
        out_specs=[vmem] * 3,
        scratch_shapes=[
            pltpu.VMEM((2, group, width), jnp.bfloat16),
            pltpu.VMEM((2, group, width), jnp.bfloat16),
            pltpu.VMEM((group, group), f32),
            pltpu.VMEM((chunk, group), jnp.bfloat16),
            pltpu.VMEM((chunk, width), f32),
            pltpu.VMEM((8, group), f32),
            pltpu.VMEM((group, 128), f32),
            pltpu.VMEM((8, group), f32),
            pltpu.VMEM((2, n_z, 8, 256), f32),
            pltpu.VMEM((2, tok, feat * n_z), jnp.bfloat16),
            pltpu.VMEM((n_z, packed, 128), jnp.bfloat16),
            pltpu.VMEM((n_z, packed, 128), jnp.bfloat16),
            pltpu.VMEM((group, feat), jnp.bfloat16),
            pltpu.VMEM((2, slab, width), f32),
            pltpu.VMEM((feat, width), f32),
            pltpu.VMEM((slab, width), f32),
            pltpu.VMEM((n_x, slab, 2 * rank), f32),
            pltpu.VMEM((n_y, slab, 2 * rank), f32),
            pltpu.VMEM((n_z, rank // 2, 2 * rank), f32),
            pltpu.VMEM((n_rep, 8, width // 2), f32),
            pltpu.VMEM((n_rep, 8, width // 2), f32),
            pltpu.VMEM((n_z, 8, width // 2), f32),
            pltpu.VMEM((n_rep, 8, width // 2), f32),
            pltpu.VMEM((n_rep, 8, width // 2), f32),
            pltpu.VMEM((rank, rank), f32),
            pltpu.VMEM((rank, rank), f32),
            pltpu.VMEM((rank, rank), f32),
            pltpu.VMEM((rank, rank), f32),
            pltpu.VMEM((2, rank, slab), f32),
            pltpu.VMEM((rank, slab), f32),
            dma((2, 8)), dma((2, 8)),
            dma((2, 9)), dma((2, 9)),
            dma((2, 4)), dma((2, 4)),
            dma((n_z,)), dma((n_z,)),
            dma((3,)), dma((3,)),
            dma((4,)),
            dma((n_x,)), dma((n_x,)),
            dma((n_y,)), dma((n_y,)),
            dma((n_z,)), dma((n_z,)),
            dma((n_rep,)), dma((n_rep,)),
            dma((n_z,)), dma((n_z,)),
            dma((n_rep,)), dma((n_rep,)),
            dma((4,)), dma((4,)),
        ],
        compiler_params=pltpu.CompilerParams(
            collective_id=0, has_side_effects=True, vmem_limit_bytes=63 * 1024 * 1024
        ),
        name="whole",
    )(proj_a, proj_b, labels, hidden_a, hidden_b, err_a, err_b, seed)


def update_kernel(p, q, mem, p_a, q_a, new_a, p_b, q_b, new_b):
    for head, outs in enumerate(((p_a, q_a, new_a), (p_b, q_b, new_b))):
        outs[0][...] = p[head]
        outs[1][...] = q[head]
        outs[2][0] = mem[head] - exact(p[head], q[head], TN)


def update(p, q, mem):
    vmem = pl.BlockSpec(memory_space=pltpu.VMEM)
    shapes = (p.shape[1:], q.shape[1:], (1,) + mem.shape[1:]) * 2
    return pl.pallas_call(
        update_kernel,
        out_shape=tuple(jax.ShapeDtypeStruct(shape, jnp.float32) for shape in shapes),
        in_specs=[vmem] * 3,
        out_specs=[vmem] * 6,
        compiler_params=pltpu.CompilerParams(vmem_limit_bytes=16 * 1024 * 1024),
        name="update",
    )(p, q, mem)


def shards(
    audio_hidden, score_hidden, audio_proj, score_proj, labels, q_seed, err_audio, err_score
):
    n_z = 8
    n_y = n_x = 4
    p, q, mem = whole(
        n_y, n_x, n_z, audio_proj, score_proj, labels, audio_hidden, score_hidden,
        err_audio, err_score, q_seed.T,
    )
    p_a, q_a, new_a, p_b, q_b, new_b = update(p, q, mem)
    return (p_a.T, q_a.T, new_a, p_b.T, q_b.T, new_b)


def solution(mesh):
    placed = (
        P(("rep", "con"), None),
        P(("rep", "con"), None),
        P(("rep", "con"), None),
        P(("rep", "con"), None),
        P("rep", "con"),
        P(),
        P("rep", "con", None),
        P("rep", "con", None),
    )
    return jax.shard_map(
        shards,
        mesh=mesh,
        in_specs=placed,
        out_specs=(
            P("con", None),
            P(),
            P("rep", "con", None),
            P("con", None),
            P(),
            P("rep", "con", None),
        ),
        check_vma=False,
    )
```

```python
import functools

import jax
import jax.numpy as jnp
from jax import lax
from jax.experimental import pallas as pl
from jax.experimental.pallas import tpu as pltpu
from jax.sharding import PartitionSpec as P

MESH = pl.DeviceIdType.MESH
logit_scale = 30.0
NORM_EPS = 1e-06
LOG2E = 1.4426950408889634
NT = (((1,), (1,)), ((), ()))
TN = (((0,), (0,)), ((), ()))
NN = (((1,), (0,)), ((), ()))
HIGH = lax.Precision.HIGHEST

SLOT_OF = (0, 1, 3, 5, 7, 6, 4, 2)
BEHIND = (0, 1, 7, 2, 6, 3, 5, 4)
RING = (
    ((1, 0), (1, 1), (2, 0), (2, 1), (3, 0), (3, 1), (4, 0), (4, 0)),
    ((1, 1), (1, 0), (2, 1), (2, 0), (3, 1), (3, 0), (4, 1), (4, 1)),
)
FAR = 7


def exact(left, right, dims):
    return lax.dot_general(
        left, right, dims, precision=HIGH, preferred_element_type=jnp.float32
    )


OWN = 8

BOUNDS = ((0, 0), (960, 768), (1600, 1536), (2240, 2048), (2400, 2304), (2560, 2560))
ROW_TILE = (480, 400, 560, 600, 640)
COL_TILE = (0, 768, 512, 512, 768)


def whole_kernel(
    n_y, n_x, n_z, proj_a, proj_b, labels, hidden_a, hidden_b, err_a, err_b, seed,
    p_ref, q_ref, mem_ref,
    raw, emb, logit, weight, grad, col_sum, row_info, col_id, lab, pair, stage, blocks,
    hid, err, mem, mem_sib, x_buf, y_buf, g_buf, part, gathered, z_buf, full, full_sib,
    coeff, resid, basis, basis_sib, p_own, p_sib,
    ring_send, ring_recv, sib_send, sib_recv, lab_send, lab_recv, hid_send, hid_recv,
    near_send, near_recv, local_sem,
    x_send, x_recv, y_send, y_recv, g_send, g_recv, r_send, r_recv, z_send, z_recv,
    f_send, f_recv, pair_send, pair_recv,
):
    n_rep = n_y * n_x
    rank, width = seed.shape
    tok = proj_a.shape[0]
    chip = 2 * tok
    group = raw.shape[1]
    feat = hid.shape[1]
    slab = err_a.shape[1]
    rep = lax.axis_index("rep")
    con = lax.axis_index("con")
    y = rep // n_x
    x = lax.rem(rep, n_x)
    z = con // 2
    core = lax.rem(con, 2)
    other = 1 - core

    def plane(ahead):
        return (rep, lax.rem(z + ahead, n_z) * 2 + core)

    sibling = (rep, z * 2 + other)

    def along_x(i):
        return (y * n_x + lax.rem(x + i, n_x), con)

    def along_y(i):
        return (lax.rem(y + i, n_y) * n_x + x, con)

    def along_rep(i):
        return (lax.rem(rep + i, n_rep), con)

    projs = (proj_a, proj_b)
    loads = [
        pltpu.make_async_copy(projs[t], raw.at[t, pl.ds(0, tok), :], local_sem.at[t])
        for t in range(2)
    ]
    for load in loads:
        load.start()

    lab[0, 0] = jnp.zeros(lab.shape[2:], jnp.float32)
    lab[0, 0, :, 0:tok] = jnp.broadcast_to(labels[...].astype(jnp.float32), (8, tok))

    barrier = pltpu.get_barrier_semaphore()
    greet = [plane(1), plane(n_z - 1), sibling]
    greet += [along_x(i) for i in range(1, n_x)] + [along_y(i) for i in range(1, n_y)]
    for peer in greet:
        pl.semaphore_signal(barrier, inc=1, device_id=peer, device_id_type=MESH)
    pl.semaphore_wait(barrier, len(greet))
    for load in loads:
        load.wait()

    def remote(source, target, send, recv, peer):
        return pltpu.make_async_remote_copy(
            src_ref=source, dst_ref=target, send_sem=send, recv_sem=recv,
            device_id=peer, device_id_type=MESH,
        )

    def slot_at(way, dist):
        return SLOT_OF[dist] if way == 0 else SLOT_OF[(n_z - dist) % n_z]

    half = tok // 2

    def place(slot, cross, part):
        if slot == FAR:
            return slot * chip + (part * 2 + cross) * half, half
        return slot * chip + cross * tok, tok

    def item(way, n):
        dist, t = RING[way][n]
        return dist, t, slot_at(way, dist), (n - 6 if dist == 4 else 0)

    def ring(way, n):
        dist, t, slot, part = item(way, n)
        first, rows = place(slot, 0, part)
        source = place(slot_at(way, dist - 1), 0, 0)[0] + part * half
        return remote(
            raw.at[t, pl.ds(source, rows), :],
            raw.at[t, pl.ds(first, rows), :],
            ring_send.at[way, n],
            ring_recv.at[way, n],
            plane(1 if way == 0 else n_z - 1),
        )

    def sib(way, n):
        dist, t, slot, part = item(way, n) if n < OWN else (0, way, 0, 0)
        first, rows = place(slot, 0, part)
        target, _ = place(slot, 1, part)
        return remote(
            raw.at[t, pl.ds(first, rows), :],
            raw.at[t, pl.ds(target, rows), :],
            sib_send.at[way, n],
            sib_recv.at[way, n],
            sibling,
        )

    def lab_copy(way, dist):
        return remote(
            lab.at[0, slot_at(way, dist - 1)], lab.at[0, slot_at(way, dist)],
            lab_send.at[way, dist - 1], lab_recv.at[way, dist - 1],
            plane(1 if way == 0 else n_z - 1),
        )

    def hid_copy(o):
        return remote(
            stage.at[lax.rem(z + o, n_z)], blocks.at[SLOT_OF[o]],
            hid_send.at[o], hid_recv.at[o], plane(o),
        )

    def lab_near():
        return remote(lab.at[0], lab.at[1], near_send.at[0], near_recv.at[0], sibling)

    def hid_near(source):
        return remote(source, pair.at[1], near_send.at[1], near_recv.at[1], sibling)

    def err_near(source):
        return remote(source.at[0], err.at[1], near_send.at[2], near_recv.at[2], sibling)

    def hid_local(source):
        return pltpu.make_async_copy(source, pair.at[0], local_sem.at[2])

    def err_local(source):
        return pltpu.make_async_copy(source.at[0], err.at[0], local_sem.at[3])

    def normalize(slot, cross, t, part=0):
        first, count = place(slot, cross, part)
        rows = pl.ds(first, count)
        values = raw[t, rows, :].astype(jnp.float32)
        inverse = lax.rsqrt(jnp.sum(values * values, axis=1, keepdims=True) + NORM_EPS)
        emb[t, rows, :] = (values * inverse).astype(jnp.bfloat16)
        row_info[rows, t : t + 1] = inverse

    for way in range(2):
        lab_copy(way, 1).start()
    for n in range(2):
        for way in range(2):
            ring(way, n).start()
    for t in range(2):
        sib(t, OWN).start()

    @pl.when(core == 0)
    def _():
        hid_near(hidden_b).start()
        hid_local(hidden_a).start()
        err_near(err_b).start()
        err_local(err_a).start()

    @pl.when(core == 1)
    def _():
        hid_near(hidden_a).start()
        hid_local(hidden_b).start()
        err_near(err_a).start()
        err_local(err_b).start()

    row_info[...] = jnp.zeros_like(row_info)
    col_sum[...] = jnp.zeros_like(col_sum)
    for t in range(2):
        normalize(0, 0, t)
    for t in range(2):
        sib(t, OWN).wait_recv()
        normalize(0, 1, t)

    def tile_logits(r0, rows, c0, cols):
        left = emb[core, pl.ds(r0, rows), :]
        right = emb[other, pl.ds(c0, cols), :]
        part = jnp.exp2(
            (logit_scale * LOG2E)
            * lax.dot_general(left, right, NT, preferred_element_type=jnp.float32)
        )
        logit[pl.ds(r0, rows), pl.ds(c0, cols)] = part
        lanes = part[:, 0:128]
        for k in range(1, cols // 128):
            lanes = lanes + part[:, k * 128 : (k + 1) * 128]
        row_info[pl.ds(r0, rows), 6:7] += jnp.sum(lanes, axis=1, keepdims=True)
        col_sum[:, pl.ds(c0, cols)] += jnp.sum(part.reshape(rows // 8, 8, cols), axis=0)

    def logits_step(step):
        old_rows, old_cols = BOUNDS[step]
        new_rows, new_cols = BOUNDS[step + 1]
        cols = new_cols - old_cols
        rows = ROW_TILE[step]

        def columns(k, _):
            tile_logits(pl.multiple_of(k * rows, 16), rows, old_cols, cols)
            return 0

        def more(k, _):
            first = pl.multiple_of(k * COL_TILE[step], 256)
            tile_logits(old_rows, new_rows - old_rows, first, COL_TILE[step])
            return 0

        if step < 2:
            lax.fori_loop(0, new_rows // rows, columns, 0)
        else:
            for k in range(new_rows // rows):
                tile_logits(k * rows, rows, old_cols, cols)
        if step == 1:
            lax.fori_loop(0, old_cols // COL_TILE[step], more, 0)
        elif step > 2:
            for k in range(old_cols // COL_TILE[step]):
                tile_logits(old_rows, new_rows - old_rows, k * COL_TILE[step], COL_TILE[step])

    def late_rows(which):
        first = pl.multiple_of(5 * chip + which * chip, 16)
        for k in range(BOUNDS[2][1] // COL_TILE[2]):
            tile_logits(first, chip, k * COL_TILE[2], COL_TILE[2])

    wide = stage.shape[2]
    narrow = feat - wide
    part_rows = chip * narrow // wide

    def pack():
        for half in range(2):
            for k in range(n_z):
                first = k * feat
                stage[k, half * tok : (half + 1) * tok, :] = pair[half, :, first : first + wide]
                for g in range(tok // part_rows):
                    lane = (half * (tok // part_rows) + g) * narrow
                    stage[k, chip : chip + part_rows, lane : lane + narrow] = pair[
                        half, g * part_rows : (g + 1) * part_rows, first + wide : first + feat
                    ]

    def unpack(slot, block):
        for g in range(chip // part_rows):
            cross, part = g // 2, g % 2
            first = place(slot, cross, part)[0] + (0 if slot == FAR else part * half)
            source = slice(g * part_rows, (g + 1) * part_rows)
            hid[first : first + part_rows, 0:wide] = block[source, :]
            hid[first : first + part_rows, wide:feat] = block[
                chip : chip + part_rows, g * narrow : (g + 1) * narrow
            ]

    def pair_ids():
        for slot in range(n_z):
            where = lax.rem(z + n_z - BEHIND[slot], n_z)
            for r in range(2):
                first = ((where * 2 + (other if r else core)) * tok).astype(jnp.float32)
                piece = lab[r, slot]
                spread = jnp.broadcast_to(piece[0:1, :], (128, piece.shape[1])).T[:tok, 0:1]
                own = first + lax.broadcasted_iota(jnp.int32, (tok, 1), 0).astype(jnp.float32)
                ids_row = jnp.where(core == 0, spread, own)
                ids_col = jnp.where(core == 0, own, spread)
                for part in range(2):
                    start = place(slot, r, part)[0] + (0 if slot == FAR else part * half)
                    source = slice(part * half, (part + 1) * half)
                    row_info[start : start + half, 2:3] = ids_row[source, :]
                    row_info[start : start + half, 3:4] = ids_col[source, :]
        for k in range(group // 128):
            ids = row_info[k * 128 : (k + 1) * 128, 3:4]
            col_id[:, k * 128 : (k + 1) * 128] = jnp.broadcast_to(ids, (128, 128)).T[0:8, :]

    last = len(RING[0])

    def forward(n):
        for way in range(2):
            ring(way, n).wait_recv()
            if n < (4, 3)[way]:
                lab_copy(way, n + 1).wait_recv()
            if n + 2 <= (4, 3)[way]:
                lab_copy(way, n + 2).start()
            if n < 5:
                ring(way, n + 2).start()
            if n == 5:
                ring(way, 7).start()
            sib(way, n).start()

    def arrived(n, cross):
        for way in range(2):
            _, t, slot, end = item(way, n)
            if cross:
                sib(way, n).wait_recv()
            normalize(slot, cross, t, end)

    for n in range(6):
        forward(n)
        arrived(n, 0)
        if n == 0:
            hid_near(hidden_a).wait_recv()
            hid_local(hidden_a).wait()
            pack()
        if n == 3:
            lab_near().start()
        arrived(n, 1)
        if n in (1, 3):
            logits_step(n // 2)
        if n == 4:
            lab_near().wait_recv()
            pair_ids()
            late_rows(core)
    late_rows(other)
    forward(6)
    for o in range(1, n_z):
        hid_copy(o).start()
    arrived(6, 0)
    logits_step(2)
    forward(7)
    arrived(7, 0)
    arrived(6, 1)
    logits_step(3)
    arrived(7, 1)
    logits_step(4)

    row_info[:, 4:5] = 0.5 / row_info[:, 6:7]
    col_sum[0:1, :] = 0.5 / jnp.sum(col_sum[...], axis=0, keepdims=True)
    row_info[:, 5:6] = jnp.where(core == 0, row_info[:, 0:1], row_info[:, 1:2])

    chunk = weight.shape[0]
    fine = 16

    def chunk_step(k, _):
        r0 = pl.multiple_of(k * chunk, chunk)
        for m in range(chunk // fine):
            rows = pl.ds(r0 + m * fine, fine)
            value = logit[rows, :] * (row_info[rows, 4:5] + col_sum[0:1, :])
            value = value - jnp.where(row_info[rows, 2:3] == col_id[0:1, :], 1.0, 0.0)
            weight[m * fine : (m + 1) * fine, :] = value.astype(jnp.bfloat16)
        grad[...] = lax.dot_general(
            weight[...], emb[other], NN, preferred_element_type=jnp.float32
        )
        for m in range(chunk // fine):
            rows = pl.ds(r0 + m * fine, fine)
            inverse = row_info[rows, 5:6]
            unit = raw[core, rows, :].astype(jnp.float32) * inverse
            value = logit_scale * grad[m * fine : (m + 1) * fine, :]
            along = jnp.sum(unit * value, axis=1, keepdims=True)
            emb[core, rows, :] = ((value - unit * along) * inverse).astype(jnp.bfloat16)
        return 0

    lax.fori_loop(0, group // chunk, chunk_step, 0)
    for o in range(1, n_z):
        hid_copy(o).wait_recv()
    err_near(err_a).wait_recv()
    err_local(err_a).wait()
    unpack(0, stage.at[z])
    for o in range(1, n_z):
        unpack(SLOT_OF[o], blocks.at[SLOT_OF[o]])
    total = lax.dot_general(hid[...], emb[core], TN, preferred_element_type=jnp.float32)
    for k in range(2):
        rows = slice(k * slab, (k + 1) * slab)
        mem[rows, :] = total[rows, :] + err[jnp.where(core == k, 0, 1)]

    theirs = pl.ds(pl.multiple_of(other * slab, 8), slab)
    ours = pl.ds(pl.multiple_of(core * slab, 8), slab)
    mem_copy = remote(mem.at[theirs, :], mem_sib, pair_send.at[0], pair_recv.at[0], sibling)
    mem_copy.start()

    def all_sum(buf, index, count, send, recv, peers, value):
        buf[index] = value
        copies = [
            remote(buf.at[index], buf.at[index], send.at[i], recv.at[i], peers(i))
            for i in range(1, count)
        ]
        for one in copies:
            one.start()

        def finish():
            for one in copies:
                one.wait()
            total = buf[0]
            for k in range(1, count):
                total = total + buf[k]
            return total

        return finish

    left = exact(seed[...], mem[...], NT)
    strip = rank // 4
    packed = jnp.concatenate(
        [left[:, :128]]
        + [jnp.concatenate([left[g * strip : (g + 1) * strip, 128:] for g in range(4)], axis=1)],
        axis=0,
    )
    packed = all_sum(x_buf, x, n_x, x_send, x_recv, along_x, packed)()
    packed = all_sum(y_buf, y, n_y, y_send, y_recv, along_y, packed)()
    tail = [packed[rank:, g * 32 : (g + 1) * 32] for g in range(4)]
    left = jnp.concatenate([packed[:rank, :], jnp.concatenate(tail, axis=0)], axis=1)

    right = exact(left, mem[...], NN)
    span = width // 2
    for k in range(n_rep):
        part[k] = right[8 * (k // 2) : 8 * (k // 2) + 8, span * (k % 2) : span * (k % 2) + span]
    gathered[rep] = part[rep]
    reduce = [
        remote(
            part.at[lax.rem(rep + i, n_rep)], gathered.at[rep], r_send.at[i], r_recv.at[i],
            along_rep(i),
        )
        for i in range(1, n_rep)
    ]
    for one in reduce:
        one.start()

    gram = exact(left, left, NT)
    gram_sum = all_sum(
        g_buf, z, n_z, g_send, g_recv, plane,
        jnp.concatenate([gram[: rank // 2, :], gram[rank // 2 :, :]], axis=1),
    )

    for one in reduce:
        one.wait()
    total = gathered[0]
    for k in range(1, n_rep):
        total = total + gathered[k]
    z_sum = all_sum(z_buf, z, n_z, z_send, z_recv, plane, total)

    gram = gram_sum()
    resid[...] = jnp.concatenate([gram[:, :rank], gram[:, rank:]], axis=0)
    coeff[...] = (
        lax.broadcasted_iota(jnp.int32, (rank, rank), 0)
        == lax.broadcasted_iota(jnp.int32, (rank, rank), 1)
    ).astype(jnp.float32)

    def column_step(k, _):
        lane = lax.broadcasted_iota(jnp.int32, (rank, rank), 1)
        u = coeff[pl.ds(k, 1), :]
        w = resid[pl.ds(k, 1), :]
        values = resid[...]
        square = jnp.maximum(jnp.sum(u * w, axis=1, keepdims=True), 0.0) + NORM_EPS
        column = jnp.sum(jnp.where(lane == k, values, 0.0), axis=1, keepdims=True)
        inverse = 1.0 / square
        basis[pl.ds(k, 1), :] = u * lax.rsqrt(square)
        coeff[...] -= column * (u * inverse)
        resid[...] = values - column * (w * inverse)
        return 0

    lax.fori_loop(0, rank // 2, column_step, 0)
    full[rep] = z_sum()
    spread = [
        remote(full.at[rep], full.at[rep], f_send.at[i], f_recv.at[i], along_rep(i))
        for i in range(1, n_rep)
    ]
    for one in spread:
        one.start()
    lax.fori_loop(rank // 2, rank, column_step, 0)

    turn_copy = remote(basis, basis_sib, pair_send.at[2], pair_recv.at[2], sibling)
    turn_copy.start()
    turn = basis[...]
    factor = exact(turn, left, NN)
    for k in range(2):
        p_own[k] = factor[:, k * slab : (k + 1) * slab]
    p_copy = remote(p_own.at[other], p_sib, pair_send.at[1], pair_recv.at[1], sibling)
    p_copy.start()
    for one in spread:
        one.wait_recv()
    full_copy = remote(full, full_sib, pair_send.at[3], pair_recv.at[3], sibling)
    full_copy.start()

    def finish(head, turn, blocks, memory, factor):
        right = jnp.concatenate(
            [
                jnp.concatenate([blocks[2 * k], blocks[2 * k + 1]], axis=1)
                for k in range(n_rep // 2)
            ],
            axis=0,
        )
        right = exact(turn, right, NN) / n_rep
        q_ref[head] = right
        p_ref[head] = factor
        mem_ref[head] = memory

    finish(core, turn, full, mem[ours, :], p_own[core])
    mem_copy.wait()
    p_copy.wait()
    turn_copy.wait()
    full_copy.wait()
    finish(other, basis_sib[...], full_sib, mem_sib[...], p_sib[...])
    for one in spread:
        one.wait_send()

    for way in range(2):
        for n in range(last):
            ring(way, n).wait_send()
        for n in range(last + 1):
            sib(way, n).wait_send()
        for dist in range(1, (5, 4)[way]):
            lab_copy(way, dist).wait_send()
    for o in range(1, n_z):
        hid_copy(o).wait_send()
    lab_near().wait_send()
    hid_near(hidden_a).wait_send()
    err_near(err_a).wait_send()


def whole(n_y, n_x, n_z, proj_a, proj_b, labels, hidden_a, hidden_b, err_a, err_b, seed):
    tok, width = proj_a.shape
    rank = seed.shape[0]
    group = tok * n_z * 2
    feat = hidden_a.shape[1] // n_z
    slab = err_a.shape[1]
    n_rep = n_y * n_x
    chunk = 256
    packed = 2 * tok * feat // 128
    dma = pltpu.SemaphoreType.DMA
    any_space = pl.BlockSpec(memory_space=pl.ANY)
    vmem = pl.BlockSpec(memory_space=pltpu.VMEM)
    f32 = jnp.float32
    return pl.pallas_call(
        functools.partial(whole_kernel, n_y, n_x, n_z),
        out_shape=(
            jax.ShapeDtypeStruct((2, rank, slab), f32),
            jax.ShapeDtypeStruct((2, rank, width), f32),
            jax.ShapeDtypeStruct((2, slab, width), f32),
        ),
        in_specs=[any_space, any_space, vmem] + [any_space] * 4 + [vmem],
        out_specs=[vmem] * 3,
        scratch_shapes=[
            pltpu.VMEM((2, group, width), jnp.bfloat16),
            pltpu.VMEM((2, group, width), jnp.bfloat16),
            pltpu.VMEM((group, group), f32),
            pltpu.VMEM((chunk, group), jnp.bfloat16),
            pltpu.VMEM((chunk, width), f32),
            pltpu.VMEM((8, group), f32),
            pltpu.VMEM((group, 128), f32),
            pltpu.VMEM((8, group), f32),
            pltpu.VMEM((2, n_z, 8, 256), f32),
            pltpu.VMEM((2, tok, feat * n_z), jnp.bfloat16),
            pltpu.VMEM((n_z, packed, 128), jnp.bfloat16),
            pltpu.VMEM((n_z, packed, 128), jnp.bfloat16),
            pltpu.VMEM((group, feat), jnp.bfloat16),
            pltpu.VMEM((2, slab, width), f32),
            pltpu.VMEM((feat, width), f32),
            pltpu.VMEM((slab, width), f32),
            pltpu.VMEM((n_x, slab, 2 * rank), f32),
            pltpu.VMEM((n_y, slab, 2 * rank), f32),
            pltpu.VMEM((n_z, rank // 2, 2 * rank), f32),
            pltpu.VMEM((n_rep, 8, width // 2), f32),
            pltpu.VMEM((n_rep, 8, width // 2), f32),
            pltpu.VMEM((n_z, 8, width // 2), f32),
            pltpu.VMEM((n_rep, 8, width // 2), f32),
            pltpu.VMEM((n_rep, 8, width // 2), f32),
            pltpu.VMEM((rank, rank), f32),
            pltpu.VMEM((rank, rank), f32),
            pltpu.VMEM((rank, rank), f32),
            pltpu.VMEM((rank, rank), f32),
            pltpu.VMEM((2, rank, slab), f32),
            pltpu.VMEM((rank, slab), f32),
            dma((2, 8)), dma((2, 8)),
            dma((2, 9)), dma((2, 9)),
            dma((2, 4)), dma((2, 4)),
            dma((n_z,)), dma((n_z,)),
            dma((3,)), dma((3,)),
            dma((4,)),
            dma((n_x,)), dma((n_x,)),
            dma((n_y,)), dma((n_y,)),
            dma((n_z,)), dma((n_z,)),
            dma((n_rep,)), dma((n_rep,)),
            dma((n_z,)), dma((n_z,)),
            dma((n_rep,)), dma((n_rep,)),
            dma((4,)), dma((4,)),
        ],
        compiler_params=pltpu.CompilerParams(
            collective_id=0, has_side_effects=True, vmem_limit_bytes=63 * 1024 * 1024
        ),
        name="whole",
    )(proj_a, proj_b, labels, hidden_a, hidden_b, err_a, err_b, seed)


def update_kernel(p, q, mem, p_a, q_a, new_a, p_b, q_b, new_b):
    for head, outs in enumerate(((p_a, q_a, new_a), (p_b, q_b, new_b))):
        outs[0][...] = p[head]
        outs[1][...] = q[head]
        outs[2][0] = mem[head] - exact(p[head], q[head], TN)


def update(p, q, mem):
    vmem = pl.BlockSpec(memory_space=pltpu.VMEM)
    shapes = (p.shape[1:], q.shape[1:], (1,) + mem.shape[1:]) * 2
    return pl.pallas_call(
        update_kernel,
        out_shape=tuple(jax.ShapeDtypeStruct(shape, jnp.float32) for shape in shapes),
        in_specs=[vmem] * 3,
        out_specs=[vmem] * 6,
        compiler_params=pltpu.CompilerParams(vmem_limit_bytes=60 * 1024 * 1024),
        name="update",
    )(p, q, mem)


def shards(
    audio_hidden, score_hidden, audio_proj, score_proj, labels, q_seed, err_audio, err_score
):
    n_z = 8
    n_y = n_x = 4
    p, q, mem = whole(
        n_y, n_x, n_z, audio_proj, score_proj, labels, audio_hidden, score_hidden,
        err_audio, err_score, q_seed.T,
    )
    p_a, q_a, new_a, p_b, q_b, new_b = update(p, q, mem)
    return (p_a.T, q_a.T, new_a, p_b.T, q_b.T, new_b)


def solution(mesh):
    placed = (
        P(("rep", "con"), None),
        P(("rep", "con"), None),
        P(("rep", "con"), None),
        P(("rep", "con"), None),
        P("rep", "con"),
        P(),
        P("rep", "con", None),
        P("rep", "con", None),
    )
    return jax.shard_map(
        shards,
        mesh=mesh,
        in_specs=placed,
        out_specs=(
            P("con", None),
            P(),
            P("rep", "con", None),
            P("con", None),
            P(),
            P("rep", "con", None),
        ),
        check_vma=False,
    )
```

```python
import functools

import jax
import jax.numpy as jnp
from jax import lax
from jax.experimental import pallas as pl
from jax.experimental.pallas import tpu as pltpu
from jax.sharding import PartitionSpec as P

MESH = pl.DeviceIdType.MESH
logit_scale = 30.0
NORM_EPS = 1e-06
LOG2E = 1.4426950408889634
NT = (((1,), (1,)), ((), ()))
TN = (((0,), (0,)), ((), ()))
NN = (((1,), (0,)), ((), ()))
HIGH = lax.Precision.HIGHEST

SLOT_OF = (0, 1, 3, 5, 7, 6, 4, 2)
BEHIND = (0, 1, 7, 2, 6, 3, 5, 4)
RING = (
    ((1, 0), (1, 1), (2, 0), (2, 1), (3, 0), (3, 1), (4, 0), (4, 0)),
    ((1, 1), (1, 0), (2, 1), (2, 0), (3, 1), (3, 0), (4, 1), (4, 1)),
)
FAR = 7


def exact(left, right, dims):
    return lax.dot_general(
        left, right, dims, precision=HIGH, preferred_element_type=jnp.float32
    )


OWN = 8

BOUNDS = ((0, 0), (960, 768), (1600, 1536), (2240, 2048), (2400, 2304), (2560, 2560))
ROW_TILE = (480, 400, 560, 600, 640)
COL_TILE = (0, 768, 512, 512, 768)


def whole_kernel(
    n_y, n_x, n_z, proj_a, proj_b, labels, hidden_a, hidden_b, err_a, err_b, seed,
    p_ref, q_ref, mem_ref,
    raw, emb, logit, weight, grad, col_sum, row_info, col_id, lab, pair, stage, blocks,
    hid, err, mem, mem_sib, x_buf, y_buf, g_buf, part, gathered, z_buf, full, full_sib,
    coeff, resid, basis, basis_sib, p_own, p_sib,
    ring_send, ring_recv, sib_send, sib_recv, lab_send, lab_recv, hid_send, hid_recv,
    near_send, near_recv, local_sem,
    x_send, x_recv, y_send, y_recv, g_send, g_recv, r_send, r_recv, z_send, z_recv,
    f_send, f_recv, pair_send, pair_recv,
):
    n_rep = n_y * n_x
    rank, width = seed.shape
    tok = proj_a.shape[0]
    chip = 2 * tok
    group = raw.shape[1]
    feat = hid.shape[1]
    slab = err_a.shape[1]
    rep = lax.axis_index("rep")
    con = lax.axis_index("con")
    y = rep // n_x
    x = lax.rem(rep, n_x)
    z = con // 2
    core = lax.rem(con, 2)
    other = 1 - core

    def plane(ahead):
        return (rep, lax.rem(z + ahead, n_z) * 2 + core)

    sibling = (rep, z * 2 + other)

    def along_x(i):
        return (y * n_x + lax.rem(x + i, n_x), con)

    def along_y(i):
        return (lax.rem(y + i, n_y) * n_x + x, con)

    def along_rep(i):
        return (lax.rem(rep + i, n_rep), con)

    projs = (proj_a, proj_b)
    loads = [
        pltpu.make_async_copy(projs[t], raw.at[t, pl.ds(0, tok), :], local_sem.at[t])
        for t in range(2)
    ]
    for load in loads:
        load.start()

    lab[0, 0] = jnp.zeros(lab.shape[2:], jnp.float32)
    lab[0, 0, :, 0:tok] = jnp.broadcast_to(labels[...].astype(jnp.float32), (8, tok))

    barrier = pltpu.get_barrier_semaphore()
    greet = [plane(1), plane(n_z - 1), sibling]
    greet += [along_x(i) for i in range(1, n_x)] + [along_y(i) for i in range(1, n_y)]
    for peer in greet:
        pl.semaphore_signal(barrier, inc=1, device_id=peer, device_id_type=MESH)
    pl.semaphore_wait(barrier, len(greet))
    for load in loads:
        load.wait()

    def remote(source, target, send, recv, peer):
        return pltpu.make_async_remote_copy(
            src_ref=source, dst_ref=target, send_sem=send, recv_sem=recv,
            device_id=peer, device_id_type=MESH,
        )

    def slot_at(way, dist):
        return SLOT_OF[dist] if way == 0 else SLOT_OF[(n_z - dist) % n_z]

    half = tok // 2

    def place(slot, cross, part):
        if slot == FAR:
            return slot * chip + (part * 2 + cross) * half, half
        return slot * chip + cross * tok, tok

    def item(way, n):
        dist, t = RING[way][n]
        return dist, t, slot_at(way, dist), (n - 6 if dist == 4 else 0)

    def ring(way, n):
        dist, t, slot, part = item(way, n)
        first, rows = place(slot, 0, part)
        source = place(slot_at(way, dist - 1), 0, 0)[0] + part * half
        return remote(
            raw.at[t, pl.ds(source, rows), :],
            raw.at[t, pl.ds(first, rows), :],
            ring_send.at[way, n],
            ring_recv.at[way, n],
            plane(1 if way == 0 else n_z - 1),
        )

    def sib(way, n):
        dist, t, slot, part = item(way, n) if n < OWN else (0, way, 0, 0)
        first, rows = place(slot, 0, part)
        target, _ = place(slot, 1, part)
        return remote(
            raw.at[t, pl.ds(first, rows), :],
            raw.at[t, pl.ds(target, rows), :],
            sib_send.at[way, n],
            sib_recv.at[way, n],
            sibling,
        )

    def lab_copy(way, dist):
        return remote(
            lab.at[0, slot_at(way, dist - 1)], lab.at[0, slot_at(way, dist)],
            lab_send.at[way, dist - 1], lab_recv.at[way, dist - 1],
            plane(1 if way == 0 else n_z - 1),
        )

    def hid_copy(o):
        return remote(
            stage.at[lax.rem(z + o, n_z)], blocks.at[SLOT_OF[o]],
            hid_send.at[o], hid_recv.at[o], plane(o),
        )

    def lab_near():
        return remote(lab.at[0], lab.at[1], near_send.at[0], near_recv.at[0], sibling)

    def hid_near(source):
        return remote(source, pair.at[1], near_send.at[1], near_recv.at[1], sibling)

    def err_near(source):
        return remote(source.at[0], err.at[1], near_send.at[2], near_recv.at[2], sibling)

    def hid_local(source):
        return pltpu.make_async_copy(source, pair.at[0], local_sem.at[2])

    def err_local(source):
        return pltpu.make_async_copy(source.at[0], err.at[0], local_sem.at[3])

    def normalize(slot, cross, t, part=0):
        first, count = place(slot, cross, part)
        rows = pl.ds(first, count)
        values = raw[t, rows, :].astype(jnp.float32)
        inverse = lax.rsqrt(jnp.sum(values * values, axis=1, keepdims=True) + NORM_EPS)
        emb[t, rows, :] = (values * inverse).astype(jnp.bfloat16)
        row_info[rows, t : t + 1] = inverse

    for way in range(2):
        lab_copy(way, 1).start()
    for n in range(2):
        for way in range(2):
            ring(way, n).start()
    for t in range(2):
        sib(t, OWN).start()

    @pl.when(core == 0)
    def _():
        hid_near(hidden_b).start()
        hid_local(hidden_a).start()
        err_near(err_b).start()
        err_local(err_a).start()

    @pl.when(core == 1)
    def _():
        hid_near(hidden_a).start()
        hid_local(hidden_b).start()
        err_near(err_a).start()
        err_local(err_b).start()

    row_info[...] = jnp.zeros_like(row_info)
    col_sum[...] = jnp.zeros_like(col_sum)
    for t in range(2):
        normalize(0, 0, t)
    for t in range(2):
        sib(t, OWN).wait_recv()
        normalize(0, 1, t)

    def tile_logits(r0, rows, c0, cols):
        left = emb[core, pl.ds(r0, rows), :]
        right = emb[other, pl.ds(c0, cols), :]
        part = jnp.exp2(
            (logit_scale * LOG2E)
            * lax.dot_general(left, right, NT, preferred_element_type=jnp.float32)
        )
        logit[pl.ds(r0, rows), pl.ds(c0, cols)] = part
        lanes = part[:, 0:128]
        for k in range(1, cols // 128):
            lanes = lanes + part[:, k * 128 : (k + 1) * 128]
        row_info[pl.ds(r0, rows), 6:7] += jnp.sum(lanes, axis=1, keepdims=True)
        col_sum[:, pl.ds(c0, cols)] += jnp.sum(part.reshape(rows // 8, 8, cols), axis=0)

    def logits_step(step):
        old_rows, old_cols = BOUNDS[step]
        new_rows, new_cols = BOUNDS[step + 1]
        cols = new_cols - old_cols
        rows = ROW_TILE[step]

        def columns(k, _):
            tile_logits(pl.multiple_of(k * rows, 16), rows, old_cols, cols)
            return 0

        def more(k, _):
            first = pl.multiple_of(k * COL_TILE[step], 256)
            tile_logits(old_rows, new_rows - old_rows, first, COL_TILE[step])
            return 0

        if step < 2:
            lax.fori_loop(0, new_rows // rows, columns, 0)
        else:
            for k in range(new_rows // rows):
                tile_logits(k * rows, rows, old_cols, cols)
        if step == 1:
            lax.fori_loop(0, old_cols // COL_TILE[step], more, 0)
        elif step > 2:
            for k in range(old_cols // COL_TILE[step]):
                tile_logits(old_rows, new_rows - old_rows, k * COL_TILE[step], COL_TILE[step])

    def late_rows(which):
        first = pl.multiple_of(5 * chip + which * chip, 16)
        for k in range(BOUNDS[2][1] // COL_TILE[2]):
            tile_logits(first, chip, k * COL_TILE[2], COL_TILE[2])

    wide = stage.shape[2]
    narrow = feat - wide
    part_rows = chip * narrow // wide

    def pack():
        for half in range(2):
            for k in range(n_z):
                first = k * feat
                stage[k, half * tok : (half + 1) * tok, :] = pair[half, :, first : first + wide]
                for g in range(tok // part_rows):
                    lane = (half * (tok // part_rows) + g) * narrow
                    stage[k, chip : chip + part_rows, lane : lane + narrow] = pair[
                        half, g * part_rows : (g + 1) * part_rows, first + wide : first + feat
                    ]

    def unpack(slot, block):
        for g in range(chip // part_rows):
            cross, part = g // 2, g % 2
            first = place(slot, cross, part)[0] + (0 if slot == FAR else part * half)
            source = slice(g * part_rows, (g + 1) * part_rows)
            hid[first : first + part_rows, 0:wide] = block[source, :]
            hid[first : first + part_rows, wide:feat] = block[
                chip : chip + part_rows, g * narrow : (g + 1) * narrow
            ]

    def pair_ids():
        for slot in range(n_z):
            where = lax.rem(z + n_z - BEHIND[slot], n_z)
            for r in range(2):
                first = ((where * 2 + (other if r else core)) * tok).astype(jnp.float32)
                piece = lab[r, slot]
                spread = jnp.broadcast_to(piece[0:1, :], (128, piece.shape[1])).T[:tok, 0:1]
                own = first + lax.broadcasted_iota(jnp.int32, (tok, 1), 0).astype(jnp.float32)
                ids_row = jnp.where(core == 0, spread, own)
                ids_col = jnp.where(core == 0, own, spread)
                for part in range(2):
                    start = place(slot, r, part)[0] + (0 if slot == FAR else part * half)
                    source = slice(part * half, (part + 1) * half)
                    row_info[start : start + half, 2:3] = ids_row[source, :]
                    row_info[start : start + half, 3:4] = ids_col[source, :]
        for k in range(group // 128):
            ids = row_info[k * 128 : (k + 1) * 128, 3:4]
            col_id[:, k * 128 : (k + 1) * 128] = jnp.broadcast_to(ids, (128, 128)).T[0:8, :]

    last = len(RING[0])

    def forward(n):
        for way in range(2):
            ring(way, n).wait_recv()
            if n < (4, 3)[way]:
                lab_copy(way, n + 1).wait_recv()
            if n + 2 <= (4, 3)[way]:
                lab_copy(way, n + 2).start()
            if n < 5:
                ring(way, n + 2).start()
            if n == 5:
                ring(way, 7).start()
            sib(way, n).start()

    def arrived(n, cross):
        for way in range(2):
            _, t, slot, end = item(way, n)
            if cross:
                sib(way, n).wait_recv()
            normalize(slot, cross, t, end)

    for n in range(6):
        forward(n)
        arrived(n, 0)
        if n == 0:
            hid_near(hidden_a).wait_recv()
            hid_local(hidden_a).wait()
            pack()
        if n == 3:
            lab_near().start()
        arrived(n, 1)
        if n in (1, 3):
            logits_step(n // 2)
        if n == 4:
            lab_near().wait_recv()
            pair_ids()
            late_rows(core)
    late_rows(other)
    forward(6)
    for o in range(1, n_z):
        hid_copy(o).start()
    arrived(6, 0)
    logits_step(2)
    forward(7)
    arrived(7, 0)
    arrived(6, 1)
    logits_step(3)
    arrived(7, 1)
    logits_step(4)

    row_info[:, 4:5] = 0.5 / row_info[:, 6:7]
    col_sum[0:1, :] = 0.5 / jnp.sum(col_sum[...], axis=0, keepdims=True)
    row_info[:, 5:6] = jnp.where(core == 0, row_info[:, 0:1], row_info[:, 1:2])

    chunk = weight.shape[0]
    fine = 16

    def chunk_step(k, _):
        r0 = pl.multiple_of(k * chunk, chunk)
        for m in range(chunk // fine):
            rows = pl.ds(r0 + m * fine, fine)
            value = logit[rows, :] * (row_info[rows, 4:5] + col_sum[0:1, :])
            value = value - jnp.where(row_info[rows, 2:3] == col_id[0:1, :], 1.0, 0.0)
            weight[m * fine : (m + 1) * fine, :] = value.astype(jnp.bfloat16)
        grad[...] = lax.dot_general(
            weight[...], emb[other], NN, preferred_element_type=jnp.float32
        )
        for m in range(chunk // fine):
            rows = pl.ds(r0 + m * fine, fine)
            inverse = row_info[rows, 5:6]
            unit = raw[core, rows, :].astype(jnp.float32) * inverse
            value = logit_scale * grad[m * fine : (m + 1) * fine, :]
            along = jnp.sum(unit * value, axis=1, keepdims=True)
            emb[core, rows, :] = ((value - unit * along) * inverse).astype(jnp.bfloat16)
        return 0

    lax.fori_loop(0, group // chunk, chunk_step, 0)
    for o in range(1, n_z):
        hid_copy(o).wait_recv()
    err_near(err_a).wait_recv()
    err_local(err_a).wait()
    unpack(0, stage.at[z])
    for o in range(1, n_z):
        unpack(SLOT_OF[o], blocks.at[SLOT_OF[o]])
    total = lax.dot_general(hid[...], emb[core], TN, preferred_element_type=jnp.float32)
    for k in range(2):
        rows = slice(k * slab, (k + 1) * slab)
        mem[rows, :] = total[rows, :] + err[jnp.where(core == k, 0, 1)]

    theirs = pl.ds(pl.multiple_of(other * slab, 8), slab)
    ours = pl.ds(pl.multiple_of(core * slab, 8), slab)
    mem_copy = remote(mem.at[theirs, :], mem_sib, pair_send.at[0], pair_recv.at[0], sibling)
    mem_copy.start()

    def all_sum(buf, index, count, send, recv, peers, value):
        buf[index] = value
        copies = [
            remote(buf.at[index], buf.at[index], send.at[i], recv.at[i], peers(i))
            for i in range(1, count)
        ]
        for one in copies:
            one.start()

        def finish():
            for one in copies:
                one.wait()
            total = buf[0]
            for k in range(1, count):
                total = total + buf[k]
            return total

        return finish

    left = exact(seed[...], mem[...], NT)
    strip = rank // 4
    packed = jnp.concatenate(
        [left[:, :128]]
        + [jnp.concatenate([left[g * strip : (g + 1) * strip, 128:] for g in range(4)], axis=1)],
        axis=0,
    )
    middle = packed.shape[0] // 2

    def over_x(k, value):
        return all_sum(x_buf.at[k], x, n_x, x_send.at[k], x_recv.at[k], along_x, value)

    def over_y(k, value):
        return all_sum(y_buf.at[k], y, n_y, y_send.at[k], y_recv.at[k], along_y, value)

    top, low = over_x(0, packed[:middle]), over_y(1, packed[middle:])
    top = over_y(0, top())
    low = over_x(1, low())
    packed = jnp.concatenate([top(), low()], axis=0)
    tail = [packed[rank:, g * 32 : (g + 1) * 32] for g in range(4)]
    left = jnp.concatenate([packed[:rank, :], jnp.concatenate(tail, axis=0)], axis=1)

    right = exact(left, mem[...], NN)
    span = width // 2
    for k in range(n_rep):
        part[k] = right[8 * (k // 2) : 8 * (k // 2) + 8, span * (k % 2) : span * (k % 2) + span]
    gathered[rep] = part[rep]
    reduce = [
        remote(
            part.at[lax.rem(rep + i, n_rep)], gathered.at[rep], r_send.at[i], r_recv.at[i],
            along_rep(i),
        )
        for i in range(1, n_rep)
    ]
    for one in reduce:
        one.start()

    gram = exact(left, left, NT)
    gram_sum = all_sum(
        g_buf, z, n_z, g_send, g_recv, plane,
        jnp.concatenate([gram[: rank // 2, :], gram[rank // 2 :, :]], axis=1),
    )

    for one in reduce:
        one.wait()
    total = gathered[0]
    for k in range(1, n_rep):
        total = total + gathered[k]
    z_sum = all_sum(z_buf, z, n_z, z_send, z_recv, plane, total)

    gram = gram_sum()
    resid[...] = jnp.concatenate([gram[:, :rank], gram[:, rank:]], axis=0)
    coeff[...] = (
        lax.broadcasted_iota(jnp.int32, (rank, rank), 0)
        == lax.broadcasted_iota(jnp.int32, (rank, rank), 1)
    ).astype(jnp.float32)

    def column_step(k, _):
        lane = lax.broadcasted_iota(jnp.int32, (rank, rank), 1)
        u = coeff[pl.ds(k, 1), :]
        w = resid[pl.ds(k, 1), :]
        values = resid[...]
        square = jnp.maximum(jnp.sum(u * w, axis=1, keepdims=True), 0.0) + NORM_EPS
        column = jnp.sum(jnp.where(lane == k, values, 0.0), axis=1, keepdims=True)
        inverse = 1.0 / square
        basis[pl.ds(k, 1), :] = u * lax.rsqrt(square)
        coeff[...] -= column * (u * inverse)
        resid[...] = values - column * (w * inverse)
        return 0

    lax.fori_loop(0, rank // 2, column_step, 0)
    full[rep] = z_sum()
    spread = [
        remote(full.at[rep], full.at[rep], f_send.at[i], f_recv.at[i], along_rep(i))
        for i in range(1, n_rep)
    ]
    for one in spread:
        one.start()
    lax.fori_loop(rank // 2, rank, column_step, 0)

    turn_copy = remote(basis, basis_sib, pair_send.at[2], pair_recv.at[2], sibling)
    turn_copy.start()
    turn = basis[...]
    factor = exact(turn, left, NN)
    for k in range(2):
        p_own[k] = factor[:, k * slab : (k + 1) * slab]
    p_copy = remote(p_own.at[other], p_sib, pair_send.at[1], pair_recv.at[1], sibling)
    p_copy.start()
    for one in spread:
        one.wait_recv()
    full_copy = remote(full, full_sib, pair_send.at[3], pair_recv.at[3], sibling)
    full_copy.start()

    def finish(head, turn, blocks, memory, factor):
        right = jnp.concatenate(
            [
                jnp.concatenate([blocks[2 * k], blocks[2 * k + 1]], axis=1)
                for k in range(n_rep // 2)
            ],
            axis=0,
        )
        right = exact(turn, right, NN) / n_rep
        q_ref[head] = right
        p_ref[head] = factor
        mem_ref[head] = memory

    finish(core, turn, full, mem[ours, :], p_own[core])
    mem_copy.wait()
    p_copy.wait()
    turn_copy.wait()
    full_copy.wait()
    finish(other, basis_sib[...], full_sib, mem_sib[...], p_sib[...])
    for one in spread:
        one.wait_send()

    for way in range(2):
        for n in range(last):
            ring(way, n).wait_send()
        for n in range(last + 1):
            sib(way, n).wait_send()
        for dist in range(1, (5, 4)[way]):
            lab_copy(way, dist).wait_send()
    for o in range(1, n_z):
        hid_copy(o).wait_send()
    lab_near().wait_send()
    hid_near(hidden_a).wait_send()
    err_near(err_a).wait_send()


def whole(n_y, n_x, n_z, proj_a, proj_b, labels, hidden_a, hidden_b, err_a, err_b, seed):
    tok, width = proj_a.shape
    rank = seed.shape[0]
    group = tok * n_z * 2
    feat = hidden_a.shape[1] // n_z
    slab = err_a.shape[1]
    n_rep = n_y * n_x
    chunk = 256
    packed = 2 * tok * feat // 128
    dma = pltpu.SemaphoreType.DMA
    any_space = pl.BlockSpec(memory_space=pl.ANY)
    vmem = pl.BlockSpec(memory_space=pltpu.VMEM)
    f32 = jnp.float32
    return pl.pallas_call(
        functools.partial(whole_kernel, n_y, n_x, n_z),
        out_shape=(
            jax.ShapeDtypeStruct((2, rank, slab), f32),
            jax.ShapeDtypeStruct((2, rank, width), f32),
            jax.ShapeDtypeStruct((2, slab, width), f32),
        ),
        in_specs=[any_space, any_space, vmem] + [any_space] * 4 + [vmem],
        out_specs=[vmem] * 3,
        scratch_shapes=[
            pltpu.VMEM((2, group, width), jnp.bfloat16),
            pltpu.VMEM((2, group, width), jnp.bfloat16),
            pltpu.VMEM((group, group), f32),
            pltpu.VMEM((chunk, group), jnp.bfloat16),
            pltpu.VMEM((chunk, width), f32),
            pltpu.VMEM((8, group), f32),
            pltpu.VMEM((group, 128), f32),
            pltpu.VMEM((8, group), f32),
            pltpu.VMEM((2, n_z, 8, 256), f32),
            pltpu.VMEM((2, tok, feat * n_z), jnp.bfloat16),
            pltpu.VMEM((n_z, packed, 128), jnp.bfloat16),
            pltpu.VMEM((n_z, packed, 128), jnp.bfloat16),
            pltpu.VMEM((group, feat), jnp.bfloat16),
            pltpu.VMEM((2, slab, width), f32),
            pltpu.VMEM((feat, width), f32),
            pltpu.VMEM((slab, width), f32),
            pltpu.VMEM((2, n_x, slab // 2, 2 * rank), f32),
            pltpu.VMEM((2, n_y, slab // 2, 2 * rank), f32),
            pltpu.VMEM((n_z, rank // 2, 2 * rank), f32),
            pltpu.VMEM((n_rep, 8, width // 2), f32),
            pltpu.VMEM((n_rep, 8, width // 2), f32),
            pltpu.VMEM((n_z, 8, width // 2), f32),
            pltpu.VMEM((n_rep, 8, width // 2), f32),
            pltpu.VMEM((n_rep, 8, width // 2), f32),
            pltpu.VMEM((rank, rank), f32),
            pltpu.VMEM((rank, rank), f32),
            pltpu.VMEM((rank, rank), f32),
            pltpu.VMEM((rank, rank), f32),
            pltpu.VMEM((2, rank, slab), f32),
            pltpu.VMEM((rank, slab), f32),
            dma((2, 8)), dma((2, 8)),
            dma((2, 9)), dma((2, 9)),
            dma((2, 4)), dma((2, 4)),
            dma((n_z,)), dma((n_z,)),
            dma((3,)), dma((3,)),
            dma((4,)),
            dma((2, n_x)), dma((2, n_x)),
            dma((2, n_y)), dma((2, n_y)),
            dma((n_z,)), dma((n_z,)),
            dma((n_rep,)), dma((n_rep,)),
            dma((n_z,)), dma((n_z,)),
            dma((n_rep,)), dma((n_rep,)),
            dma((4,)), dma((4,)),
        ],
        compiler_params=pltpu.CompilerParams(
            collective_id=0, has_side_effects=True, vmem_limit_bytes=63 * 1024 * 1024
        ),
        name="whole",
    )(proj_a, proj_b, labels, hidden_a, hidden_b, err_a, err_b, seed)


def update_kernel(p, q, mem, p_a, q_a, new_a, p_b, q_b, new_b):
    for head, outs in enumerate(((p_a, q_a, new_a), (p_b, q_b, new_b))):
        outs[0][...] = p[head]
        outs[1][...] = q[head]
        outs[2][0] = mem[head] - exact(p[head], q[head], TN)


def update(p, q, mem):
    vmem = pl.BlockSpec(memory_space=pltpu.VMEM)
    shapes = (p.shape[1:], q.shape[1:], (1,) + mem.shape[1:]) * 2
    return pl.pallas_call(
        update_kernel,
        out_shape=tuple(jax.ShapeDtypeStruct(shape, jnp.float32) for shape in shapes),
        in_specs=[vmem] * 3,
        out_specs=[vmem] * 6,
        compiler_params=pltpu.CompilerParams(vmem_limit_bytes=60 * 1024 * 1024),
        name="update",
    )(p, q, mem)


def shards(
    audio_hidden, score_hidden, audio_proj, score_proj, labels, q_seed, err_audio, err_score
):
    n_z = 8
    n_y = n_x = 4
    p, q, mem = whole(
        n_y, n_x, n_z, audio_proj, score_proj, labels, audio_hidden, score_hidden,
        err_audio, err_score, q_seed.T,
    )
    p_a, q_a, new_a, p_b, q_b, new_b = update(p, q, mem)
    return (p_a.T, q_a.T, new_a, p_b.T, q_b.T, new_b)


def solution(mesh):
    placed = (
        P(("rep", "con"), None),
        P(("rep", "con"), None),
        P(("rep", "con"), None),
        P(("rep", "con"), None),
        P("rep", "con"),
        P(),
        P("rep", "con", None),
        P("rep", "con", None),
    )
    return jax.shard_map(
        shards,
        mesh=mesh,
        in_specs=placed,
        out_specs=(
            P("con", None),
            P(),
            P("rep", "con", None),
            P("con", None),
            P(),
            P("rep", "con", None),
        ),
        check_vma=False,
    )
```
